256 devices in a mesh: seq: 8 (over y_hi, x), chan: 32 (over z, y_lo, core).
Axes of the slice: x: 4, y: 4 (y_hi: 2, y_lo: 2; y = y_hi * 2 + y_lo), z: 8, core: 2. Of those that a mesh axis runs over, the one named last changes fastest.
Arguments:
- tokens: bfloat16 [1024, 8192], P('seq', 'chan'), may hold values from -11 to 11
- norm_gain: bfloat16 [8192], P('chan'), may hold values from 0.099609375 to 1.8984375
- in_weight: bfloat16 [8192, 3, 4096], P(None, None, 'chan'), may hold values from -0.0625 to 0.0625
- short_filter: float32 [3, 3, 4096], P(None, None, 'chan'), may hold values from -3 to 3
- prior_rows: bfloat16 [2, 3, 4096], P(None, None, 'chan'), may hold values from -5 to 5
- decay_rate: float32 [4096, 16], P('chan'), may hold values from 0.0001953125 to 0.05
- pole_angle: float32 [4096, 16], P('chan'), may hold values from -3.140625 to 3.140625
- residue: float32 [2, 4096, 16], P(None, 'chan'), may hold values from -0.32 to 0.32
- prior_state: float32 [2, 4096, 16], P(None, 'chan'), may hold values from -202.38577 to 202.38577
- skip_weight: float32 [4096], P('chan'), may hold values from -3 to 3
- out_weight: bfloat16 [4096, 8192], P(None, 'chan'), may hold values from -0.09375 to 0.09375
Outputs:
- mixed: bfloat16 [1024, 8192], P('seq', 'chan')
The draws below stay inside these ranges and needn't reach their ends.
All inputs are finite; a program needn't handle non-finite values.
Results may differ from the reference program's by a relative error of at most 0.0083.
Values may be sent and summed in bfloat16 or wider, within the bound.
A program may use at most 64 MiB of HBM per device.

```python
import math
import jax
import jax.numpy as jnp
from jax import lax

D = 8192
MODES = 16
C = 4096
SHORT = 3
TOKENS = 1024


def modal_rates(key):
    keys = jax.random.split(jax.random.fold_in(key, 7), 3)
    share = 0.5
    slow = jax.random.uniform(keys[0], (C, MODES)) < share
    slow_rate = jnp.exp(jax.random.uniform(keys[1], (C, MODES), minval=math.log(0.2 / TOKENS), maxval=math.log(2.0 / TOKENS)))
    fast_rate = jnp.exp(jax.random.uniform(keys[2], (C, MODES), minval=math.log(0.02), maxval=math.log(0.05)))
    return jnp.where(slow, slow_rate, fast_rate).astype(jnp.float32)


def bounded_noise(key):
    return jnp.clip(jax.random.normal(key, (2, C, MODES)), -4.0, 4.0)


def draw_tokens(key, part):
    keys = jax.random.split(key, 3)
    row_scale = jnp.exp(jax.random.uniform(keys[0], (TOKENS, 1), minval=math.log(0.3), maxval=math.log(3.0)))
    column_scale = jnp.exp(jax.random.uniform(keys[1], (1, D), minval=math.log(0.3), maxval=math.log(3.0)))
    noise = jnp.clip(jax.random.normal(keys[2], (TOKENS, D)), -4.0, 4.0)
    return jnp.clip(0.3 * noise * row_scale * column_scale, -11.0, 11.0).astype(jnp.bfloat16)


def draw_decay_rate(key, part):
    return modal_rates(key)


def draw_residue(key, part):
    rates = modal_rates(key)
    noise = bounded_noise(jax.random.fold_in(key, 8))
    return noise * jnp.sqrt(2.0 * rates / MODES)[None]


def draw_prior_state(key, part):
    rates = modal_rates(key)
    noise = bounded_noise(jax.random.fold_in(key, 9))
    return noise * jnp.sqrt(0.5 / rates)[None]


def block_scale(own_key, extent, pieces, least, largest):
    def one(position, parts):
        draws = jax.random.uniform(jax.random.fold_in(jax.random.fold_in(own_key, 6), position), (parts,), jnp.float32, least / len(pieces), largest / len(pieces))
        return jnp.repeat(jnp.exp(draws), extent[position] // parts).reshape((-1,) + (1,) * (len(extent) - position - 1))

    gain = one(*pieces[0])
    for cut in pieces[1:]:
        gain = gain * one(*cut)
    return gain


def bell_draw(key, dims, spread, reach, pieces=(), dtype=jnp.bfloat16):
    factor_of = block_scale(key, dims, pieces, -0.22, 0.18) if pieces else 1.0
    drawn = jax.random.normal(key, dims, jnp.float32) * spread * factor_of
    return jnp.minimum(jnp.maximum(drawn, -reach), reach).astype(dtype)


def setup_inputs(seed: int = 0) -> dict:
    streams_of = jax.random.split(jax.random.key(seed), 12)
    return {
        "tokens": draw_tokens(jax.random.fold_in(streams_of[11], 71), 0),
        "norm_gain": jnp.clip(1.0 + 0.18 * jax.random.normal(streams_of[1], (D,), jnp.float32), 0.099609375, 1.8984375).astype(jnp.bfloat16),
        "in_weight": bell_draw(streams_of[2], (D, 3, C), D ** -0.5, 0.0625, ((2, 32),)),
        "short_filter": bell_draw(streams_of[3], (SHORT, 3, C), 0.6, 3.0, ((2, 32),), jnp.float32),
        "prior_rows": bell_draw(streams_of[4], (SHORT - 1, 3, C), 1.0, 5.0, ((2, 32),)),
        "decay_rate": draw_decay_rate(jax.random.fold_in(streams_of[11], 71), 0),
        "pole_angle": jnp.clip(jax.random.uniform(streams_of[6], (C, MODES), jnp.float32, -3.140625, 3.140625), -3.140625, 3.140625),
        "residue": draw_residue(jax.random.fold_in(streams_of[11], 71), 0),
        "prior_state": draw_prior_state(jax.random.fold_in(streams_of[11], 71), 0),
        "skip_weight": bell_draw(streams_of[9], (C,), 0.5, 3.0, ((0, 32),), jnp.float32),
        "out_weight": bell_draw(streams_of[10], (C, D), C ** -0.5, 0.09375, ((1, 32),)),
    }


EPSILON = 1e-06

def reference(tokens, norm_gain, in_weight, short_filter, prior_rows, decay_rate, pole_angle, residue, prior_state, skip_weight, out_weight):
    values = tokens.astype(jnp.float32)
    scale = lax.rsqrt(lax.optimization_barrier(jnp.mean(values * values, axis=1)) + EPSILON)
    normed = (values * scale[:, None] * norm_gain.astype(jnp.float32)[None, :]).astype(jnp.bfloat16)
    width = 3 * C
    projected = jnp.dot(normed, in_weight.reshape(D, width), preferred_element_type=jnp.float32).astype(jnp.bfloat16)
    margin = SHORT - 1
    extended = jnp.concatenate([prior_rows.reshape(margin, width), projected], axis=0).astype(jnp.float32)
    taps = short_filter.reshape(SHORT, width)
    convolved = jnp.zeros((TOKENS, width), jnp.float32)
    for lag in range(SHORT):
        convolved = convolved + taps[lag][None, :] * extended[margin - lag:margin - lag + TOKENS]
    convolved = convolved.reshape(TOKENS, 3, C)
    query_rows = convolved[:, 0, :]
    drive = convolved[:, 1, :] * convolved[:, 2, :]
    magnitude = jnp.exp(-decay_rate)
    pole_real = magnitude * jnp.cos(pole_angle)
    pole_imaginary = magnitude * jnp.sin(pole_angle)

    def advance(state, row):
        real_part, imaginary_part = state
        new_real = pole_real * real_part - pole_imaginary * imaginary_part + row[:, None]
        new_imaginary = pole_real * imaginary_part + pole_imaginary * real_part
        output = lax.optimization_barrier(jnp.sum(residue[0] * new_real - residue[1] * new_imaginary, axis=1))
        return ((new_real, new_imaginary), output)
    final_state, mode_out = lax.scan(advance, (prior_state[0], prior_state[1]), drive)
    gated = (query_rows * (mode_out + skip_weight[None, :] * drive)).astype(jnp.bfloat16)
    summed = jnp.dot(gated, out_weight, preferred_element_type=jnp.float32)
    return (values + summed).astype(jnp.bfloat16)
```

```python
import jax
import jax.numpy as jnp
from jax import lax
from jax.experimental import pallas as pl
from jax.experimental.pallas import tpu as pltpu
from jax.sharding import PartitionSpec as P

MESH = pl.DeviceIdType.MESH
EPSILON = 1e-06
F32 = jnp.float32
BF16 = jnp.bfloat16

Z = 8
ROWS = 128
FEATS = 256
CH = 128
MODES = 16
SEQ = 8
MESSAGES = 41


class Place:
    def __init__(self):
        self.seq = lax.axis_index("seq")
        chan = lax.axis_index("chan")
        self.chan = chan
        self.z = chan // 4
        self.y = (chan // 2) % 2
        self.k = chan % 2

    def at(self, z, y, k):
        return (self.seq, z * 4 + y * 2 + k)

    def along(self, by):
        return (self.z + by + Z) % Z


class Gather:
    def __init__(self, place, buf, own, send_sem, recv_sem):
        self.p, self.buf, self.own = place, buf, own
        self.send_sem, self.recv_sem = send_sem, recv_sem
        p = place
        self.other_y = 1 - p.y
        self.up = p.at(p.along(1), p.y, p.k)
        self.down = p.at(p.along(-1), p.y, p.k)
        self.across = p.at(p.z, 1 - p.y, p.k)
        self.core = p.at(p.z, p.y, 1 - p.k)
        self.sent = []

    def slot(self, z, y, k, rows):
        return self.buf.at[z, y, k, pl.ds(rows[0], rows[1])]

    def copy(self, src, dst, message, device):
        return pltpu.make_async_remote_copy(
            src_ref=src,
            dst_ref=dst,
            send_sem=self.send_sem.at[message],
            recv_sem=self.recv_sem.at[message],
            device_id=device,
            device_id_type=MESH,
        )

    def send(self, z, y, rows, message, device, src=None):
        here = self.slot(z, y, self.p.k, rows)
        c = self.copy(here if src is None else src.at[pl.ds(rows[0], rows[1])], here, message, device)
        c.start()
        self.sent.append(c)

    def take(self, z, y, k, rows, message):
        here = self.slot(z, y, k, rows)
        self.copy(here, here, message, self.core).wait_recv()

    def open(self):
        p, own = self.p, self.own
        self.send(p.z, p.y, (0, 64), 0, self.across, own)
        self.send(p.z, p.y, (0, 128), 2, self.up, own)
        self.send(p.z, p.y, (0, 128), 6, self.down, own)
        self.send(p.z, p.y, (64, 64), 1, self.across, own)
        self.send(p.z, p.y, (0, 128), 25, self.core, own)

    def first(self):
        p = self.p
        self.take(p.z, self.other_y, p.k, (0, 64), 0)
        self.send(p.z, self.other_y, (0, 64), 10, self.up)
        self.send(p.z, self.other_y, (0, 64), 14, self.down)
        self.take(p.z, self.other_y, p.k, (64, 64), 1)
        self.send(p.z, self.other_y, (0, 128), 26, self.core)

    def step(self, s):
        p = self.p
        ways = ((0, p.along(-s), self.up), (1, p.along(s), self.down))
        for d, z, onward in ways:
            self.take(z, p.y, p.k, (0, 128), 2 + d * 4 + s - 1)
            rows = (0, 128) if s < 3 else (64 * d, 64)
            self.send(z, p.y, rows, 2 + d * 4 + s, onward)
            self.send(z, p.y, (64, 64), 18 + d * 3 + s - 1, self.across)
            self.send(z, p.y, (0, 128), 27 + d * 3 + s - 1, self.core)
        for d, z, onward in ways:
            self.take(z, self.other_y, p.k, (0, 64), 10 + d * 4 + s - 1)
            rows = (0, 64) if s < 3 else (32 * d, 32)
            self.send(z, self.other_y, rows, 10 + d * 4 + s, onward)
        for d, z, onward in ways:
            self.take(z, self.other_y, p.k, (64, 64), 18 + d * 3 + s - 1)
            self.send(z, self.other_y, (0, 128), 34 + d * 3 + s - 1, self.core)

    def last(self):
        p = self.p
        z = p.along(4)
        self.take(z, p.y, p.k, (0, 64), 5)
        self.take(z, p.y, p.k, (64, 64), 9)
        self.send(z, p.y, (64, 64), 24, self.across)
        self.send(z, p.y, (0, 128), 33, self.core)
        self.take(z, self.other_y, p.k, (0, 32), 13)
        self.take(z, self.other_y, p.k, (32, 32), 17)
        self.take(z, self.other_y, p.k, (64, 64), 24)
        self.send(z, self.other_y, (0, 128), 40, self.core)

    def from_core(self, s, d):
        p = self.p
        z = p.along(-s if d == 0 else s)
        if s == 0:
            first, second = 25, 26
        elif s == 4:
            first, second = 33, 40
        else:
            first, second = 27 + d * 3 + s - 1, 34 + d * 3 + s - 1
        self.take(z, p.y, 1 - p.k, (0, 128), first)
        self.take(z, self.other_y, 1 - p.k, (0, 128), second)
        return z

    def close(self):
        for c in self.sent:
            c.wait_send()


def kernel(
    tokens,
    gain,
    in_weight,
    short_filter,
    prior_rows,
    decay_rate,
    pole_angle,
    residue,
    prior_state,
    skip_weight,
    out_weight,
    mixed,
    own,
    wide,
    stats,
    weight,
    narrow,
    gated,
    last_weight,
    power_re,
    power_im,
    lift_re,
    lift_im,
    response,
    total,
    edge,
    rim,
    ext,
    padded,
    ends,
    incoming,
    local_sem,
    send1,
    recv1,
    send2,
    recv2,
    small_send,
    small_recv,
):
    p = Place()
    loads = [pltpu.make_async_copy(tokens, own, local_sem.at[0])]
    for i in range(3):
        loads.append(
            pltpu.make_async_copy(in_weight.at[i], weight.at[:, pl.ds(i * CH, CH)], local_sem.at[1 + i])
        )
    loads.append(pltpu.make_async_copy(out_weight, last_weight, local_sem.at[4]))
    for c in loads:
        c.start()

    barrier = pltpu.get_barrier_semaphore()
    greeted = [p.at(p.z, p.y, 1 - p.k), p.at(p.z, 1 - p.y, p.k), p.at(p.z, 1 - p.y, 1 - p.k)]
    greeted += [p.at(p.along(i), p.y, p.k) for i in range(1, Z)]
    greeted += [((p.seq + i) % SEQ, p.chan) for i in range(1, SEQ)]
    for device in greeted:
        pl.semaphore_signal(barrier, inc=1, device_id=device, device_id_type=MESH)

    loads[0].wait()
    values = own[...].astype(F32)
    squares = jnp.sum(values * values, axis=1, keepdims=True)
    row = jnp.broadcast_to(squares, (ROWS, 128)).T
    gains = gain[...].astype(F32)
    stats[p.z, 2 * p.y + p.k] = jnp.concatenate(
        [row[0:1], gains[:, 0:128], gains[:, 128:256], row[3:8]], axis=0
    )
    wide[p.z, p.y, p.k] = own[...]

    pl.semaphore_wait(barrier, len(greeted))

    def small(src, dst, index, device):
        return pltpu.make_async_remote_copy(
            src_ref=src,
            dst_ref=dst,
            send_sem=small_send.at[index],
            recv_sem=small_recv.at[index],
            device_id=device,
            device_id_type=MESH,
        )

    small_sent = []
    mine = stats.at[p.z, 2 * p.y + p.k]
    for i, (dy, dk) in enumerate(((0, 1), (1, 0), (1, 1))):
        y = (p.y + dy) % 2
        k = (p.k + dk) % 2
        c = small(mine, mine, i, p.at(p.z, y, k))
        c.start()
        small_sent.append(c)
    spread = Gather(p, wide, own, send1, recv1)
    spread.open()
    for i, (dy, dk) in enumerate(((0, 1), (1, 0), (1, 1))):
        y = (p.y + dy) % 2
        k = (p.k + dk) % 2
        theirs = stats.at[p.z, 2 * y + k]
        small(theirs, theirs, i, p.at(p.z, y, k)).wait_recv()
    for i in range(1, Z):
        c = small(stats.at[p.z], stats.at[p.z], 2 + i, p.at(p.along(i), p.y, p.k))
        c.start()
        small_sent.append(c)
    spread.first()
    spread.step(1)

    magnitude = jnp.exp(-decay_rate[...])
    pole_re = magnitude * jnp.cos(pole_angle[...])
    pole_im = magnitude * jnp.sin(pole_angle[...])
    res_re = residue[0]
    res_im = residue[1]

    def tabulate(t, carry):
        re, im, lre, lim = carry
        power_re[t] = re
        power_im[t] = im
        response[pl.ds(t, 1)] = jnp.sum(lre, axis=0, keepdims=True)
        lre, lim = pole_re * lre - pole_im * lim, pole_re * lim + pole_im * lre
        lift_re[t] = lre
        lift_im[t] = lim
        return (pole_re * re - pole_im * im, pole_re * im + pole_im * re, lre, lim)

    one = jnp.ones((MODES, CH), F32)
    shard_re, shard_im, _, _ = lax.fori_loop(
        0, ROWS, tabulate, (one, jnp.zeros_like(one), res_re, res_im)
    )
    padded[pl.ds(0, ROWS)] = jnp.zeros((ROWS, CH), F32)
    total[...] = jnp.zeros_like(total)

    for i in range(1, Z):
        z = p.along(-i)
        small(stats.at[z], stats.at[z], 2 + i, p.at(z, p.y, p.k)).wait_recv()
    summed = jnp.zeros((1, 128), F32)
    for z in range(Z):
        for j in range(4):
            summed = summed + stats[z, j, 0:1]
    scale_row = lax.rsqrt(summed / (FEATS * 4 * Z) + EPSILON)
    scale = jnp.broadcast_to(scale_row, (ROWS, 128)).T

    def project(z):
        parts = []
        for j in range(4):
            x = wide[z, j // 2, j % 2].astype(F32)
            for h in range(2):
                part = x[:, 128 * h : 128 * h + 128] * scale * stats[z, j, 1 + h : 2 + h]
                parts.append(part.astype(BF16))
        normed = jnp.concatenate(parts, axis=1)
        rows = weight[pl.ds(pl.multiple_of(z * 4 * FEATS, 4 * FEATS), 4 * FEATS)]
        total[...] += jnp.dot(normed, rows, preferred_element_type=F32)

    for c in loads[1:4]:
        c.wait()
    spread.step(2)
    project(spread.from_core(0, 0))
    project(spread.from_core(1, 0))
    spread.step(3)
    project(spread.from_core(1, 1))
    project(spread.from_core(2, 0))
    spread.last()
    project(spread.from_core(2, 1))
    project(spread.from_core(3, 0))
    project(spread.from_core(3, 1))
    project(spread.from_core(4, 0))

    projected = total[...].astype(BF16)
    edge[...] = projected[ROWS - 16 :]
    after = ((p.seq + 1) % SEQ, p.chan)
    halo = small(edge, rim, 10, after)

    @pl.when(p.seq < SEQ - 1)
    def _():
        halo.start()

    ext[pl.ds(16, ROWS)] = projected.astype(F32)

    @pl.when(p.seq == 0)
    def _():
        for i in range(3):
            ext[pl.ds(14, 2), pl.ds(i * CH, CH)] = prior_rows[i].astype(F32)

    @pl.when(p.seq > 0)
    def _():
        halo.wait_recv()
        ext[pl.ds(0, 16)] = rim[...].astype(F32)

    convolved = []
    for i in range(3):
        lanes = pl.ds(i * CH, CH)
        c = jnp.zeros((ROWS, CH), F32)
        for lag in range(3):
            c = c + short_filter[lag, i : i + 1] * ext[pl.ds(16 - lag, ROWS), lanes]
        convolved.append(c)
    query = convolved[0]
    drive = convolved[1] * convolved[2]
    padded[pl.ds(ROWS, ROWS)] = drive

    def gather_end(i, carry):
        out = []
        for j in range(4):
            re, im = carry[j]
            t = 4 * i + j
            u = padded[pl.ds(ROWS + t, 1)]
            out.append((re + power_re[ROWS - 1 - t] * u, im + power_im[ROWS - 1 - t] * u))
        return tuple(out)

    nothing = jnp.zeros((MODES, CH), F32)
    sums = lax.fori_loop(0, ROWS // 4, gather_end, ((nothing, nothing),) * 4)
    ends[p.seq, 0] = sums[0][0] + sums[1][0] + sums[2][0] + sums[3][0]
    ends[p.seq, 1] = sums[0][1] + sums[1][1] + sums[2][1] + sums[3][1]
    here = ends.at[p.seq]
    for i in range(1, SEQ):

        @pl.when(p.seq + i < SEQ)
        def _():
            small(here, here, 10 + i, ((p.seq + i) % SEQ, p.chan)).start()

    def respond(i, acc):
        for j in range(4):
            lag = 4 * i + j
            acc = acc + response[pl.ds(lag, 1)] * padded[pl.ds(ROWS - lag, ROWS)]
        return acc

    mode_out = lax.fori_loop(0, ROWS // 4, respond, jnp.zeros((ROWS, CH), F32))

    incoming[...] = prior_state[...]
    for j in range(SEQ - 1):

        @pl.when(j < p.seq)
        def _():
            theirs = ends.at[j]
            for i in range(1, SEQ):

                @pl.when(p.seq - j == i)
                def _():
                    small(theirs, theirs, 10 + i, (j, p.chan)).wait_recv()

            re, im = incoming[0], incoming[1]
            incoming[0] = shard_re * re - shard_im * im + ends[j, 0]
            incoming[1] = shard_re * im + shard_im * re + ends[j, 1]

    in_re, in_im = incoming[0], incoming[1]
    carried = []
    for b in range(ROWS // 8):
        lre = lift_re[pl.ds(8 * b, 8)]
        lim = lift_im[pl.ds(8 * b, 8)]
        carried.append(jnp.sum(lre * in_re[None] - lim * in_im[None], axis=1))
    mode_out = mode_out + jnp.concatenate(carried, axis=0)
    gated[...] = (query * (mode_out + skip_weight[...] * drive)).astype(BF16)
    narrow[p.z, p.y, p.k] = gated[...]

    mix = Gather(p, narrow, gated, send2, recv2)
    mix.open()
    loads[4].wait()

    def output(z):
        parts = [narrow[z, j // 2, j % 2] for j in range(4)]
        rows = last_weight[pl.ds(pl.multiple_of(z * 4 * CH, 4 * CH), 4 * CH)]
        return jnp.dot(jnp.concatenate(parts, axis=1), rows, preferred_element_type=F32)

    mix.first()
    mix.step(1)
    acc = output(mix.from_core(0, 0))
    mix.step(2)
    acc = acc + output(mix.from_core(1, 0))
    acc = acc + output(mix.from_core(1, 1))
    mix.step(3)
    acc = acc + output(mix.from_core(2, 0))
    acc = acc + output(mix.from_core(2, 1))
    mix.last()
    acc = acc + output(mix.from_core(3, 0))
    acc = acc + output(mix.from_core(3, 1))
    acc = acc + output(mix.from_core(4, 0))
    mixed[...] = (own[...].astype(F32) + acc).astype(BF16)

    for c in small_sent:
        c.wait_send()
    spread.close()
    mix.close()

    @pl.when(p.seq < SEQ - 1)
    def _():
        halo.wait_send()

    for i in range(1, SEQ):

        @pl.when(p.seq + i < SEQ)
        def _():
            small(here, here, 10 + i, ((p.seq + i) % SEQ, p.chan)).wait_send()


def body(
    tokens,
    norm_gain,
    in_weight,
    short_filter,
    prior_rows,
    decay_rate,
    pole_angle,
    residue,
    prior_state,
    skip_weight,
    out_weight,
):
    vmem = pl.BlockSpec(memory_space=pltpu.VMEM)
    hbm = pl.BlockSpec(memory_space=pl.ANY)
    flops = 2 * ROWS * (FEATS * 32 * 3 * CH + CH * 32 * FEATS)
    return pl.pallas_call(
        kernel,
        out_shape=jax.ShapeDtypeStruct((ROWS, FEATS), BF16),
        in_specs=[hbm, vmem, hbm, vmem, vmem, vmem, vmem, vmem, vmem, vmem, hbm],
        out_specs=vmem,
        scratch_shapes=[
            pltpu.VMEM((ROWS, FEATS), BF16),
            pltpu.VMEM((Z, 2, 2, ROWS, FEATS), BF16),
            pltpu.VMEM((Z, 4, 8, 128), F32),
            pltpu.VMEM((Z * 4 * FEATS, 3 * CH), BF16),
            pltpu.VMEM((Z, 2, 2, ROWS, CH), BF16),
            pltpu.VMEM((ROWS, CH), BF16),
            pltpu.VMEM((Z * 4 * CH, FEATS), BF16),
            pltpu.VMEM((ROWS, MODES, CH), F32),
            pltpu.VMEM((ROWS, MODES, CH), F32),
            pltpu.VMEM((ROWS, MODES, CH), F32),
            pltpu.VMEM((ROWS, MODES, CH), F32),
            pltpu.VMEM((ROWS, CH), F32),
            pltpu.VMEM((ROWS, 3 * CH), F32),
            pltpu.VMEM((16, 3 * CH), BF16),
            pltpu.VMEM((16, 3 * CH), BF16),
            pltpu.VMEM((16 + ROWS, 3 * CH), F32),
            pltpu.VMEM((2 * ROWS, CH), F32),
            pltpu.VMEM((SEQ, 2, MODES, CH), F32),
            pltpu.VMEM((2, MODES, CH), F32),
            pltpu.SemaphoreType.DMA((5,)),
            pltpu.SemaphoreType.DMA((MESSAGES,)),
            pltpu.SemaphoreType.DMA((MESSAGES,)),
            pltpu.SemaphoreType.DMA((MESSAGES,)),
            pltpu.SemaphoreType.DMA((MESSAGES,)),
            pltpu.SemaphoreType.DMA((18,)),
            pltpu.SemaphoreType.DMA((18,)),
        ],
        compiler_params=pltpu.CompilerParams(
            collective_id=0, has_side_effects=True, vmem_limit_bytes=40 * 1024 * 1024
        ),
        cost_estimate=pl.CostEstimate(flops=flops, bytes_accessed=9 * 1024 * 1024, transcendentals=0),
    )(
        tokens,
        norm_gain.reshape(1, FEATS),
        jnp.transpose(in_weight, (1, 0, 2)),
        short_filter,
        jnp.transpose(prior_rows, (1, 0, 2)),
        decay_rate.T,
        pole_angle.T,
        jnp.transpose(residue, (0, 2, 1)),
        jnp.transpose(prior_state, (0, 2, 1)),
        skip_weight.reshape(1, CH),
        out_weight,
    )


def solution(mesh):
    return jax.shard_map(
        body,
        mesh=mesh,
        in_specs=(
            P("seq", "chan"),
            P("chan"),
            P(None, None, "chan"),
            P(None, None, "chan"),
            P(None, None, "chan"),
            P("chan", None),
            P("chan", None),
            P(None, "chan", None),
            P(None, "chan", None),
            P("chan"),
            P(None, "chan"),
        ),
        out_specs=P("seq", "chan"),
        check_vma=False,
    )
```

```python
import jax
import jax.numpy as jnp
from jax import lax
from jax.experimental import pallas as pl
from jax.experimental.pallas import tpu as pltpu
from jax.sharding import PartitionSpec as P

MESH = pl.DeviceIdType.MESH
EPSILON = 1e-06
F32 = jnp.float32
BF16 = jnp.bfloat16

Z = 8
ROWS = 128
FEATS = 256
CH = 128
MODES = 16
SEQ = 8


class Place:
    def __init__(self):
        self.seq = lax.axis_index("seq")
        chan = lax.axis_index("chan")
        self.chan = chan
        self.z = chan // 4
        self.y = (chan // 2) % 2
        self.k = chan % 2

    def at(self, z, y, k):
        return (self.seq, z * 4 + y * 2 + k)

    def to(self, dz, dy, dk):
        return self.at(self.along(dz), (self.y + dy) % 2, (self.k + dk) % 2)

    def along(self, by):
        return (self.z + by + Z) % Z


WIDE_PLAN = (
    (0, 0, 0, 128, 2, 0, 0),
    (0, 0, 0, 128, -2, 0, 0),
    (0, 0, 0, 128, 1, 0, 0),
    (0, 0, 0, 128, -1, 0, 0),
    (0, 0, 0, 128, 0, 1, 0),
    (0, 0, 0, 128, 0, 0, 1),
    "tables",
    "stats2",
    (0, 1, 64, 64, 2, 0, 0),
    (0, 1, 64, 64, -2, 0, 0),
    (0, 1, 0, 128, 0, 0, 1),
    (-2, 0, 32, 32, 2, 0, 0),
    (2, 0, 0, 32, -2, 0, 0),
    (-2, 0, 96, 32, 2, 0, 0),
    (-2, 0, 0, 96, 1, 0, 0),
    (2, 0, 0, 96, -1, 0, 0),
    (-2, 0, 0, 64, 0, 1, 0),
    (2, 0, 0, 64, 0, 1, 0),
    (-2, 0, 0, 128, 0, 0, 1),
    (2, 0, 0, 128, 0, 0, 1),
    "stats3",
    (-1, 0, 96, 32, 2, 0, 0),
    (1, 0, 64, 32, -3, 0, 0),
    (1, 0, 96, 32, -2, 0, 0),
    (-1, 0, 0, 128, 0, 1, 0),
    (1, 0, 0, 128, 0, 1, 0),
    (-1, 0, 0, 128, 0, 0, 1),
    (1, 0, 0, 128, 0, 0, 1),
    (-2, 1, 96, 32, 2, 0, 0),
    (2, 1, 64, 32, -2, 0, 0),
    (-2, 1, 0, 128, 1, 0, 0),
    (-2, 1, 0, 128, 0, 0, 1),
    (4, 0, 0, 64, 0, 1, 0),
    (2, 1, 32, 96, -1, 0, 0),
    (2, 1, 0, 128, 0, 0, 1),
    "scale",
    (3, 0, 0, 32, 0, 1, 0),
    0,
    -2,
    (-1, 1, 0, 128, 0, 0, 1),
    2,
    (-3, 0, 0, 128, 0, 0, 1),
    (4, 0, 0, 128, 0, 0, 1),
    (3, 0, 0, 128, 0, 0, 1),
    (1, 1, 0, 128, 0, 0, 1),
    -1,
    (4, 1, 0, 128, 0, 0, 1),
    (-3, 1, 0, 128, 0, 0, 1),
    (3, 1, 0, 128, 0, 0, 1),
    1,
    4,
    -3,
    3,
)

NARROW_PLAN = (
    (0, 0, 0, 128, 3, 0, 0),
    (0, 0, 0, 128, -3, 0, 0),
    (0, 0, 0, 128, 2, 0, 0),
    (0, 0, 0, 128, -2, 0, 0),
    (0, 0, 0, 128, 1, 0, 0),
    (0, 0, 0, 128, -1, 0, 0),
    (0, 0, 0, 128, 0, 1, 0),
    (0, 0, 0, 128, 0, 0, 1),
    (0, 1, 0, 128, 4, 0, 0),
    (0, 1, 0, 128, -2, 0, 0),
    (0, 1, 0, 128, 1, 0, 0),
    (0, 1, 0, 128, -1, 0, 0),
    (0, 1, 0, 128, 0, 0, 1),
    0,
    (-3, 0, 0, 128, 0, 1, 0),
    (3, 0, 0, 128, -1, 0, 0),
    (3, 0, 0, 128, 0, 1, 0),
    (-3, 0, 0, 128, 0, 0, 1),
    (3, 0, 0, 128, 0, 0, 1),
    (-2, 0, 0, 128, 0, 1, 0),
    (-2, 0, 0, 128, 0, 0, 1),
    (2, 0, 0, 128, 0, 0, 1),
    (-1, 0, 0, 128, 0, 0, 1),
    (1, 0, 0, 128, 0, 0, 1),
    (2, 1, 0, 128, 0, 0, 1),
    (-3, 1, 0, 128, 0, 0, 1),
    (1, 1, 0, 128, 0, 0, 1),
    (3, 1, 0, 128, 0, 0, 1),
    (4, 0, 0, 128, 0, 0, 1),
    2,
    (-1, 1, 0, 128, 0, 0, 1),
    (-2, 1, 0, 128, 0, 0, 1),
    -3,
    1,
    (4, 1, 0, 128, 0, 0, 1),
    3,
    -1,
    -2,
    4,
)


def nearest(dz):
    dz %= Z
    return dz - Z if dz > Z // 2 else dz


class Gather:
    def __init__(self, place, buf, plan, send_sem, recv_sem):
        self.p, self.buf, self.plan = place, buf, plan
        self.send_sem, self.recv_sem = send_sem, recv_sem
        self.sends = [step for step in plan if isinstance(step, tuple)]
        self.brings = {}
        for i, (dz, dy, first, rows, tz, ty, tk) in enumerate(self.sends):
            for r in range(first, first + rows, 16):
                self.brings[nearest(dz - tz), dy ^ ty, tk, r] = i
        self.waited = set()
        self.sent = []

    def copy(self, i, block, device):
        p = self.p
        dz, dy, dk = block
        first, rows = self.sends[i][2:4]
        here = self.buf.at[p.along(dz), (p.y + dy) % 2, (p.k + dk) % 2, pl.ds(first, rows)]
        return pltpu.make_async_remote_copy(
            src_ref=here,
            dst_ref=here,
            send_sem=self.send_sem.at[i],
            recv_sem=self.recv_sem.at[i],
            device_id=device,
            device_id_type=MESH,
        )

    def need(self, block, first, rows):
        if block == (0, 0, 0):
            return
        for r in range(first, first + rows, 16):
            i = self.brings[block + (r,)]
            if i not in self.waited:
                self.waited.add(i)
                dz, dy, _, _, tz, ty, tk = self.sends[i]
                self.copy(i, (nearest(dz - tz), dy ^ ty, tk), self.p.to(0, 0, 1)).wait_recv()

    def run(self, on_chip, named):
        for step in self.plan:
            if isinstance(step, str):
                named[step]()
            elif isinstance(step, int):
                for block in ((step, 0, 0), (step, 1, 0), (step, 0, 1), (step, 1, 1)):
                    self.need(block, 0, ROWS)
                on_chip(self.p.along(step))
            else:
                dz, dy, first, rows, tz, ty, tk = step
                self.need((nearest(dz), dy, 0), first, rows)
                c = self.copy(len(self.sent), (dz, dy, 0), self.p.to(tz, ty, tk))
                c.start()
                self.sent.append(c)

    def close(self):
        for c in self.sent:
            c.wait_send()


def kernel(
    tokens,
    gain_hbm,
    in_weight,
    filter_hbm,
    rows_hbm,
    decay_hbm,
    angle_hbm,
    residue_hbm,
    state_hbm,
    skip_hbm,
    out_weight,
    mixed,
    gain,
    short_filter,
    prior_rows,
    decay_rate,
    pole_angle,
    residue,
    skip_weight,
    own,
    wide,
    stats,
    weight,
    narrow,
    last_weight,
    power_re,
    power_im,
    lift_re,
    lift_im,
    response,
    total,
    edge,
    rim,
    ext,
    padded,
    ends,
    incoming,
    shard_power,
    scales,
    hello,
    local_sem,
    send1,
    recv1,
    send2,
    recv2,
    small_send,
    small_recv,
):
    p = Place()
    pairs = (
        (tokens, own),
        (gain_hbm, gain),
        (filter_hbm, short_filter),
        (rows_hbm, prior_rows),
        (decay_hbm, decay_rate),
        (angle_hbm, pole_angle),
        (residue_hbm, residue),
        (state_hbm, incoming),
        (skip_hbm, skip_weight),
    )
    loads = [pltpu.make_async_copy(a, b, local_sem.at[4 + i]) for i, (a, b) in enumerate(pairs)]
    weight_loads = []
    for i in range(3):
        weight_loads.append(
            pltpu.make_async_copy(in_weight.at[i], weight.at[:, pl.ds(i * CH, CH)], local_sem.at[i])
        )
    last_load = pltpu.make_async_copy(out_weight, last_weight, local_sem.at[3])
    for c in loads + weight_loads + [last_load]:
        c.start()

    barrier = pltpu.get_barrier_semaphore()
    kin = [
        (4 * (p.seq // 4) + (p.seq + 1) % 4, p.chan),
        (4 * (p.seq // 4) + (p.seq + 3) % 4, p.chan),
        ((p.seq + 4) % SEQ, p.chan),
    ]
    greeted = [p.to(*by) for by in ((0, 0, 1), (0, 1, 0), (0, 1, 1), (1, 0, 0), (-1, 0, 0), (2, 0, 0), (-2, 0, 0))]
    greeted += kin
    for device in greeted:
        pl.semaphore_signal(barrier, inc=1, device_id=device, device_id_type=MESH)

    loads[0].wait()
    loads[1].wait()
    values = own[...].astype(F32)
    squares = jnp.sum(values * values, axis=1, keepdims=True)
    row = jnp.broadcast_to(squares, (ROWS, 128)).T
    gains = gain[...].astype(F32).reshape(1, FEATS)
    stats[p.z, 2 * p.y + p.k] = jnp.concatenate(
        [row[0:1], gains[:, 0:128], gains[:, 128:256], row[3:8]], axis=0
    )
    wide[p.z, p.y, p.k] = own[...]

    pl.semaphore_wait(barrier, len(greeted))

    def small(src, dst, index, device):
        return pltpu.make_async_remote_copy(
            src_ref=src,
            dst_ref=dst,
            send_sem=small_send.at[index],
            recv_sem=small_recv.at[index],
            device_id=device,
            device_id_type=MESH,
        )

    small_sent = []

    def spread_small(src, index, device):
        c = small(src, src, index, device)
        c.start()
        small_sent.append(c)

    def small_here(z, index):
        small(stats.at[z], stats.at[z], index, p.to(0, 0, 1)).wait_recv()

    pair = ((0, 1), (1, 0), (1, 1))
    for i, (dy, dk) in enumerate(pair):
        spread_small(stats.at[p.z, 2 * p.y + p.k], i, p.to(0, dy, dk))
    for device in kin:
        pl.semaphore_signal(hello.at[0], inc=1, device_id=device, device_id_type=MESH)

    def stats2():
        for i, (dy, dk) in enumerate(pair):
            theirs = stats.at[p.z, 2 * ((p.y + dy) % 2) + (p.k + dk) % 2]
            small(theirs, theirs, i, p.to(0, dy, dk)).wait_recv()
        for i, by in enumerate((1, -1, 2, -2)):
            spread_small(stats.at[p.z], 3 + i, p.to(by, 0, 0))
        pl.semaphore_wait(hello.at[0], len(kin))
        for device in kin:
            pl.semaphore_signal(hello.at[1], inc=1, device_id=device, device_id_type=MESH)

    def stats3():
        small_here(p.along(-2), 5)
        small_here(p.along(2), 6)
        spread_small(stats.at[p.along(-2)], 7, p.to(1, 0, 0))
        spread_small(stats.at[p.along(2)], 8, p.to(-1, 0, 0))
        spread_small(stats.at[p.along(-2)], 9, p.to(2, 0, 0))

    def tables():
        for c in loads[2:]:
            c.wait()
        magnitude = jnp.exp(-decay_rate[...])
        pole_re = magnitude * jnp.cos(pole_angle[...])
        pole_im = magnitude * jnp.sin(pole_angle[...])
        res_re = residue[0]
        res_im = residue[1]

        def tabulate(t, carry):
            re, im, lre, lim = carry
            power_re[t] = re
            power_im[t] = im
            response[pl.ds(t, 1)] = jnp.sum(lre, axis=0, keepdims=True)
            lre, lim = pole_re * lre - pole_im * lim, pole_re * lim + pole_im * lre
            lift_re[t] = lre
            lift_im[t] = lim
            return (pole_re * re - pole_im * im, pole_re * im + pole_im * re, lre, lim)

        one = jnp.ones((MODES, CH), F32)
        end_re, end_im, _, _ = lax.fori_loop(
            0, ROWS, tabulate, (one, jnp.zeros_like(one), res_re, res_im)
        )
        padded[pl.ds(0, ROWS)] = jnp.zeros((ROWS, CH), F32)
        total[...] = jnp.zeros_like(total)
        shard_power[0] = end_re
        shard_power[1] = end_im

    def find_scale():
        small_here(p.along(-1), 3)
        small_here(p.along(1), 4)
        small_here(p.along(-3), 7)
        small_here(p.along(3), 8)
        small_here(p.along(4), 9)
        pl.semaphore_wait(hello.at[1], len(kin))
        summed = jnp.zeros((1, 128), F32)
        for z in range(Z):
            for j in range(4):
                summed = summed + stats[z, j, 0:1]
        scale_row = lax.rsqrt(summed / (FEATS * 4 * Z) + EPSILON)
        scales[...] = jnp.broadcast_to(scale_row, (ROWS, 128)).T
        for c in weight_loads:
            c.wait()

    def project(z):
        parts = []
        scale = scales[...]
        for j in range(4):
            x = wide[z, j // 2, j % 2].astype(F32)
            for h in range(2):
                part = x[:, 128 * h : 128 * h + 128] * scale * stats[z, j, 1 + h : 2 + h]
                parts.append(part.astype(BF16))
        normed = jnp.concatenate(parts, axis=1)
        rows = weight[pl.ds(pl.multiple_of(z * 4 * FEATS, 4 * FEATS), 4 * FEATS)]
        total[...] += jnp.dot(normed, rows, preferred_element_type=F32)

    spread = Gather(p, wide, WIDE_PLAN, send1, recv1)
    spread.run(project, {"tables": tables, "stats2": stats2, "stats3": stats3, "scale": find_scale})

    def close_spread():
        for c in small_sent:
            c.wait_send()
        spread.close()

    projected = total[...].astype(BF16)
    edge[...] = projected[ROWS - 16 :]
    after = ((p.seq + 1) % SEQ, p.chan)
    halo = small(edge, rim, 10, after)

    @pl.when(p.seq < SEQ - 1)
    def _():
        halo.start()

    ext[pl.ds(16, ROWS)] = projected.astype(F32)

    @pl.when(p.seq == 0)
    def _():
        for i in range(3):
            ext[pl.ds(14, 2), pl.ds(i * CH, CH)] = prior_rows[i].astype(F32)

    @pl.when(p.seq > 0)
    def _():
        halo.wait_recv()
        ext[pl.ds(0, 16)] = rim[...].astype(F32)

    def close_halo():
        @pl.when(p.seq < SEQ - 1)
        def _():
            halo.wait_send()

    convolved = []
    for i in range(3):
        lanes = pl.ds(i * CH, CH)
        c = jnp.zeros((ROWS, CH), F32)
        for lag in range(3):
            c = c + short_filter[lag, i : i + 1] * ext[pl.ds(16 - lag, ROWS), lanes]
        convolved.append(c)
    query = convolved[0]
    drive = convolved[1] * convolved[2]
    padded[pl.ds(ROWS, ROWS)] = drive

    def gather_end(i, carry):
        out = []
        for j in range(4):
            re, im = carry[j]
            t = 4 * i + j
            u = padded[pl.ds(ROWS + t, 1)]
            out.append((re + power_re[ROWS - 1 - t] * u, im + power_im[ROWS - 1 - t] * u))
        return tuple(out)

    nothing = jnp.zeros((MODES, CH), F32)
    sums = lax.fori_loop(0, ROWS // 4, gather_end, ((nothing, nothing),) * 4)
    ends[p.seq, 0] = sums[0][0] + sums[1][0] + sums[2][0] + sums[3][0]
    ends[p.seq, 1] = sums[0][1] + sums[1][1] + sums[2][1] + sums[3][1]
    here = ends.at[p.seq]
    for i in range(1, SEQ):

        @pl.when(p.seq + i < SEQ)
        def _():
            small(here, here, 10 + i, ((p.seq + i) % SEQ, p.chan)).start()

    def close_state():
        for i in range(1, SEQ):

            @pl.when(p.seq + i < SEQ)
            def _():
                small(here, here, 10 + i, ((p.seq + i) % SEQ, p.chan)).wait_send()

    def respond(i, acc):
        for j in range(4):
            lag = 4 * i + j
            acc = acc + response[pl.ds(lag, 1)] * padded[pl.ds(ROWS - lag, ROWS)]
        return acc

    mode_out = lax.fori_loop(0, ROWS // 4, respond, jnp.zeros((ROWS, CH), F32))

    shard_re, shard_im = shard_power[0], shard_power[1]
    for j in range(SEQ - 1):

        @pl.when(j < p.seq)
        def _():
            theirs = ends.at[j]
            for i in range(1, SEQ):

                @pl.when(p.seq - j == i)
                def _():
                    small(theirs, theirs, 10 + i, (j, p.chan)).wait_recv()

            re, im = incoming[0], incoming[1]
            incoming[0] = shard_re * re - shard_im * im + ends[j, 0]
            incoming[1] = shard_re * im + shard_im * re + ends[j, 1]

    in_re, in_im = incoming[0], incoming[1]
    carried = []
    for b in range(ROWS // 8):
        lre = lift_re[pl.ds(8 * b, 8)]
        lim = lift_im[pl.ds(8 * b, 8)]
        carried.append(jnp.sum(lre * in_re[None] - lim * in_im[None], axis=1))
    mode_out = mode_out + jnp.concatenate(carried, axis=0)
    narrow[p.z, p.y, p.k] = (query * (mode_out + skip_weight[...] * drive)).astype(BF16)

    total[:, pl.ds(0, FEATS)] = own[...].astype(F32)
    last_load.wait()

    def output(z):
        parts = [narrow[z, j // 2, j % 2] for j in range(4)]
        rows = last_weight[pl.ds(pl.multiple_of(z * 4 * CH, 4 * CH), 4 * CH)]
        total[:, pl.ds(0, FEATS)] += jnp.dot(
            jnp.concatenate(parts, axis=1), rows, preferred_element_type=F32
        )

    mix = Gather(p, narrow, NARROW_PLAN, send2, recv2)
    mix.run(output, {})
    mixed[...] = total[:, pl.ds(0, FEATS)].astype(BF16)

    mix.close()
    close_state()
    close_halo()
    close_spread()


def body(
    tokens,
    norm_gain,
    in_weight,
    short_filter,
    prior_rows,
    decay_rate,
    pole_angle,
    residue,
    prior_state,
    skip_weight,
    out_weight,
):
    vmem = pl.BlockSpec(memory_space=pltpu.VMEM)
    hbm = pl.BlockSpec(memory_space=pltpu.HBM)
    flops = 2 * ROWS * (FEATS * 32 * 3 * CH + CH * 32 * FEATS)
    return pl.pallas_call(
        kernel,
        out_shape=jax.ShapeDtypeStruct((ROWS, FEATS), BF16),
        in_specs=[hbm] * 11,
        out_specs=vmem,
        scratch_shapes=[
            pltpu.VMEM((FEATS,), BF16),
            pltpu.VMEM((3, 3, CH), F32),
            pltpu.VMEM((3, 2, CH), BF16),
            pltpu.VMEM((MODES, CH), F32),
            pltpu.VMEM((MODES, CH), F32),
            pltpu.VMEM((2, MODES, CH), F32),
            pltpu.VMEM((1, CH), F32),
            pltpu.VMEM((ROWS, FEATS), BF16),
            pltpu.VMEM((Z, 2, 2, ROWS, FEATS), BF16),
            pltpu.VMEM((Z, 4, 8, 128), F32),
            pltpu.VMEM((Z * 4 * FEATS, 3 * CH), BF16),
            pltpu.VMEM((Z, 2, 2, ROWS, CH), BF16),
            pltpu.VMEM((Z * 4 * CH, FEATS), BF16),
            pltpu.VMEM((ROWS, MODES, CH), F32),
            pltpu.VMEM((ROWS, MODES, CH), F32),
            pltpu.VMEM((ROWS, MODES, CH), F32),
            pltpu.VMEM((ROWS, MODES, CH), F32),
            pltpu.VMEM((ROWS, CH), F32),
            pltpu.VMEM((ROWS, 3 * CH), F32),
            pltpu.VMEM((16, 3 * CH), BF16),
            pltpu.VMEM((16, 3 * CH), BF16),
            pltpu.VMEM((16 + ROWS, 3 * CH), F32),
            pltpu.VMEM((2 * ROWS, CH), F32),
            pltpu.VMEM((SEQ, 2, MODES, CH), F32),
            pltpu.VMEM((2, MODES, CH), F32),
            pltpu.VMEM((2, MODES, CH), F32),
            pltpu.VMEM((ROWS, 128), F32),
            pltpu.SemaphoreType.REGULAR((2,)),
            pltpu.SemaphoreType.DMA((13,)),
            pltpu.SemaphoreType.DMA((len(WIDE_PLAN),)),
            pltpu.SemaphoreType.DMA((len(WIDE_PLAN),)),
            pltpu.SemaphoreType.DMA((len(NARROW_PLAN),)),
            pltpu.SemaphoreType.DMA((len(NARROW_PLAN),)),
            pltpu.SemaphoreType.DMA((18,)),
            pltpu.SemaphoreType.DMA((18,)),
        ],
        compiler_params=pltpu.CompilerParams(
            collective_id=0, has_side_effects=True, vmem_limit_bytes=60 * 1024 * 1024
        ),
        cost_estimate=pl.CostEstimate(flops=flops, bytes_accessed=9 * 1024 * 1024, transcendentals=0),
    )(
        tokens,
        norm_gain,
        jnp.transpose(in_weight, (1, 0, 2)),
        short_filter,
        jnp.transpose(prior_rows, (1, 0, 2)),
        decay_rate.T,
        pole_angle.T,
        jnp.transpose(residue, (0, 2, 1)),
        jnp.transpose(prior_state, (0, 2, 1)),
        skip_weight.reshape(1, CH),
        out_weight,
    )


def solution(mesh):
    return jax.shard_map(
        body,
        mesh=mesh,
        in_specs=(
            P("seq", "chan"),
            P("chan"),
            P(None, None, "chan"),
            P(None, None, "chan"),
            P(None, None, "chan"),
            P("chan", None),
            P("chan", None),
            P(None, "chan", None),
            P(None, "chan", None),
            P("chan"),
            P(None, "chan"),
        ),
        out_specs=P("seq", "chan"),
        check_vma=False,
    )
```

```python
import jax
import jax.numpy as jnp
from jax import lax
from jax.experimental import pallas as pl
from jax.experimental.pallas import tpu as pltpu
from jax.sharding import PartitionSpec as P

MESH = pl.DeviceIdType.MESH
EPSILON = 1e-06
F32 = jnp.float32
BF16 = jnp.bfloat16

Z = 8
ROWS = 128
FEATS = 256
CH = 128
MODES = 16
SEQ = 8


class Place:
    def __init__(self):
        self.seq = lax.axis_index("seq")
        chan = lax.axis_index("chan")
        self.chan = chan
        self.z = chan // 4
        self.y = (chan // 2) % 2
        self.k = chan % 2

    def at(self, z, y, k):
        return (self.seq, z * 4 + y * 2 + k)

    def to(self, dz, dy, dk):
        return self.at(self.along(dz), (self.y + dy) % 2, (self.k + dk) % 2)

    def along(self, by):
        return (self.z + by + Z) % Z


WIDE_PLAN = (
    (0, 0, 0, 128, 2, 0, 0),
    (0, 0, 0, 128, -2, 0, 0),
    (0, 0, 0, 128, 1, 0, 0),
    (0, 0, 0, 128, -1, 0, 0),
    (0, 0, 0, 128, 0, 1, 0),
    (0, 0, 0, 128, 0, 0, 1),
    "stats1",
    "tables",
    "stats2",
    (0, 1, 64, 64, 2, 0, 0),
    (0, 1, 64, 64, -2, 0, 0),
    (0, 1, 0, 128, 0, 0, 1),
    (-2, 0, 32, 32, 2, 0, 0),
    (2, 0, 0, 32, -2, 0, 0),
    (-2, 0, 96, 32, 2, 0, 0),
    (-2, 0, 0, 96, 1, 0, 0),
    (2, 0, 0, 96, -1, 0, 0),
    (-2, 0, 0, 64, 0, 1, 0),
    (2, 0, 0, 64, 0, 1, 0),
    (-2, 0, 0, 128, 0, 0, 1),
    (2, 0, 0, 128, 0, 0, 1),
    "stats3",
    (-1, 0, 96, 32, 2, 0, 0),
    (1, 0, 64, 32, -3, 0, 0),
    (1, 0, 96, 32, -2, 0, 0),
    (-1, 0, 0, 128, 0, 1, 0),
    (1, 0, 0, 128, 0, 1, 0),
    (-1, 0, 0, 128, 0, 0, 1),
    (1, 0, 0, 128, 0, 0, 1),
    (-2, 1, 96, 32, 2, 0, 0),
    (2, 1, 64, 32, -2, 0, 0),
    (-2, 1, 0, 128, 1, 0, 0),
    (-2, 1, 0, 128, 0, 0, 1),
    (4, 0, 0, 64, 0, 1, 0),
    (2, 1, 32, 96, -1, 0, 0),
    (2, 1, 0, 128, 0, 0, 1),
    "scale",
    (3, 0, 0, 32, 0, 1, 0),
    0,
    -2,
    (-1, 1, 0, 128, 0, 0, 1),
    2,
    (-3, 0, 0, 128, 0, 0, 1),
    (4, 0, 0, 128, 0, 0, 1),
    (3, 0, 0, 128, 0, 0, 1),
    (1, 1, 0, 128, 0, 0, 1),
    -1,
    (4, 1, 0, 128, 0, 0, 1),
    (-3, 1, 0, 128, 0, 0, 1),
    (3, 1, 0, 128, 0, 0, 1),
    1,
    4,
    -3,
    3,
)

NARROW_PLAN = (
    (0, 0, 0, 128, 3, 0, 0),
    (0, 0, 0, 128, -3, 0, 0),
    (0, 0, 0, 128, 2, 0, 0),
    (0, 0, 0, 128, -2, 0, 0),
    (0, 0, 0, 128, 1, 0, 0),
    (0, 0, 0, 128, -1, 0, 0),
    (0, 0, 0, 128, 0, 1, 0),
    (0, 0, 0, 128, 0, 0, 1),
    (0, 1, 0, 128, 4, 0, 0),
    (0, 1, 0, 128, -2, 0, 0),
    (0, 1, 0, 128, 1, 0, 0),
    (0, 1, 0, 128, -1, 0, 0),
    (0, 1, 0, 128, 0, 0, 1),
    0,
    (-3, 0, 0, 128, 0, 1, 0),
    (3, 0, 0, 128, -1, 0, 0),
    (3, 0, 0, 128, 0, 1, 0),
    (-3, 0, 0, 128, 0, 0, 1),
    (3, 0, 0, 128, 0, 0, 1),
    (-2, 0, 0, 128, 0, 1, 0),
    (-2, 0, 0, 128, 0, 0, 1),
    (2, 0, 0, 128, 0, 0, 1),
    (-1, 0, 0, 128, 0, 0, 1),
    (1, 0, 0, 128, 0, 0, 1),
    "settle",
    (2, 1, 0, 128, 0, 0, 1),
    (-3, 1, 0, 128, 0, 0, 1),
    (1, 1, 0, 128, 0, 0, 1),
    (3, 1, 0, 128, 0, 0, 1),
    (4, 0, 0, 128, 0, 0, 1),
    2,
    "settle",
    (-1, 1, 0, 128, 0, 0, 1),
    (-2, 1, 0, 128, 0, 0, 1),
    -3,
    1,
    (4, 1, 0, 128, 0, 0, 1),
    3,
    -1,
    -2,
    4,
)


def nearest(dz):
    dz %= Z
    return dz - Z if dz > Z // 2 else dz


class Gather:
    def __init__(self, place, buf, own, plan, send_sem, recv_sem):
        self.p, self.buf, self.own, self.plan = place, buf, own, plan
        self.send_sem, self.recv_sem = send_sem, recv_sem
        self.sends = [step for step in plan if isinstance(step, tuple)]
        self.brings = {}
        for i, (dz, dy, first, rows, tz, ty, tk) in enumerate(self.sends):
            for r in range(first, first + rows, 16):
                self.brings[nearest(dz - tz), dy ^ ty, tk, r] = i
        self.waited = set()
        self.sent = []
        self.settled = 0

    def copy(self, i, block, device):
        p = self.p
        dz, dy, dk = block
        first, rows = self.sends[i][2:4]
        here = self.buf.at[p.along(dz), (p.y + dy) % 2, (p.k + dk) % 2, pl.ds(first, rows)]
        mine = self.own is not None and block == (0, 0, 0)
        return pltpu.make_async_remote_copy(
            src_ref=self.own.at[pl.ds(first, rows)] if mine else here,
            dst_ref=here,
            send_sem=self.send_sem.at[i],
            recv_sem=self.recv_sem.at[i],
            device_id=device,
            device_id_type=MESH,
        )

    def need(self, block, first, rows):
        if block == (0, 0, 0):
            return
        for r in range(first, first + rows, 16):
            i = self.brings[block + (r,)]
            if i not in self.waited:
                self.waited.add(i)
                dz, dy, _, _, tz, ty, tk = self.sends[i]
                self.copy(i, (nearest(dz - tz), dy ^ ty, tk), self.p.to(0, 0, 1)).wait_recv()

    def run(self, on_chip, named):
        for step in self.plan:
            if isinstance(step, str):
                named[step]()
            elif isinstance(step, int):
                for block in ((step, 0, 0), (step, 1, 0), (step, 0, 1), (step, 1, 1)):
                    self.need(block, 0, ROWS)
                on_chip(self.p.along(step))
            else:
                dz, dy, first, rows, tz, ty, tk = step
                self.need((nearest(dz), dy, 0), first, rows)
                c = self.copy(len(self.sent), (dz, dy, 0), self.p.to(tz, ty, tk))
                c.start()
                self.sent.append(c)

    def settle(self, in_flight=0):
        upto = max(self.settled, len(self.sent) - in_flight)
        for c in self.sent[self.settled : upto]:
            c.wait_send()
        self.settled = upto


def kernel(
    tokens,
    gain_hbm,
    in_weight,
    filter_hbm,
    rows_hbm,
    decay_hbm,
    angle_hbm,
    residue_hbm,
    state_hbm,
    skip_hbm,
    out_weight,
    mixed,
    gain,
    short_filter,
    prior_rows,
    decay_rate,
    pole_angle,
    residue,
    skip_weight,
    own,
    wide,
    stats,
    weight,
    narrow,
    last_weight,
    power_re,
    power_im,
    lift_re,
    lift_im,
    response,
    total,
    rim,
    ext,
    padded,
    ends,
    incoming,
    shard_power,
    scales,
    hello,
    local_sem,
    send1,
    recv1,
    send2,
    recv2,
    small_send,
    small_recv,
):
    p = Place()
    barrier = pltpu.get_barrier_semaphore()
    kin = [
        (4 * (p.seq // 4) + (p.seq + 1) % 4, p.chan),
        (4 * (p.seq // 4) + (p.seq + 3) % 4, p.chan),
        ((p.seq + 4) % SEQ, p.chan),
    ]
    greeted = [p.to(*by) for by in ((0, 0, 1), (0, 1, 0), (0, 1, 1), (1, 0, 0), (-1, 0, 0), (2, 0, 0), (-2, 0, 0))]
    greeted += kin
    for device in greeted:
        pl.semaphore_signal(barrier, inc=1, device_id=device, device_id_type=MESH)

    pairs = (
        (tokens, own),
        (gain_hbm, gain),
        (filter_hbm, short_filter),
        (rows_hbm, prior_rows),
        (decay_hbm, decay_rate),
        (angle_hbm, pole_angle),
        (residue_hbm, residue),
        (state_hbm, incoming),
        (skip_hbm, skip_weight),
    )
    loads = [pltpu.make_async_copy(a, b, local_sem.at[4 + i]) for i, (a, b) in enumerate(pairs)]
    weight_loads = []
    for i in range(3):
        weight_loads.append(
            pltpu.make_async_copy(in_weight.at[i], weight.at[:, pl.ds(i * CH, CH)], local_sem.at[i])
        )
    last_load = pltpu.make_async_copy(out_weight, last_weight, local_sem.at[3])
    for c in loads + weight_loads + [last_load]:
        c.start()

    pl.semaphore_wait(barrier, len(greeted))

    def small(src, dst, index, device):
        return pltpu.make_async_remote_copy(
            src_ref=src,
            dst_ref=dst,
            send_sem=small_send.at[index],
            recv_sem=small_recv.at[index],
            device_id=device,
            device_id_type=MESH,
        )

    small_sent = []

    def spread_small(src, index, device):
        c = small(src, src, index, device)
        c.start()
        small_sent.append(c)

    def small_here(z, index):
        small(stats.at[z], stats.at[z], index, p.to(0, 0, 1)).wait_recv()

    pair = ((0, 1), (1, 0), (1, 1))

    def stats1():
        loads[0].wait()
        loads[1].wait()
        values = own[...].astype(F32)
        squares = jnp.sum(values * values, axis=1, keepdims=True)
        row = jnp.broadcast_to(squares, (ROWS, 128)).T
        gains = gain[...].astype(F32).reshape(1, FEATS)
        stats[p.z, 2 * p.y + p.k] = jnp.concatenate(
            [row[0:1], gains[:, 0:128], gains[:, 128:256], row[3:8]], axis=0
        )
        wide[p.z, p.y, p.k] = own[...]
        for i, (dy, dk) in enumerate(pair):
            spread_small(stats.at[p.z, 2 * p.y + p.k], i, p.to(0, dy, dk))
        for device in kin:
            pl.semaphore_signal(hello.at[0], inc=1, device_id=device, device_id_type=MESH)

    def stats2():
        for i, (dy, dk) in enumerate(pair):
            theirs = stats.at[p.z, 2 * ((p.y + dy) % 2) + (p.k + dk) % 2]
            small(theirs, theirs, i, p.to(0, dy, dk)).wait_recv()
        for i, by in enumerate((1, -1, 2, -2)):
            spread_small(stats.at[p.z], 3 + i, p.to(by, 0, 0))
        pl.semaphore_wait(hello.at[0], len(kin))
        for device in kin:
            pl.semaphore_signal(hello.at[1], inc=1, device_id=device, device_id_type=MESH)

    def stats3():
        small_here(p.along(-2), 5)
        small_here(p.along(2), 6)
        spread_small(stats.at[p.along(-2)], 7, p.to(1, 0, 0))
        spread_small(stats.at[p.along(2)], 8, p.to(-1, 0, 0))
        spread_small(stats.at[p.along(-2)], 9, p.to(2, 0, 0))

    def tables():
        for c in loads[2:]:
            c.wait()
        magnitude = jnp.exp(-decay_rate[...])
        pole_re = magnitude * jnp.cos(pole_angle[...])
        pole_im = magnitude * jnp.sin(pole_angle[...])
        res_re = residue[0]
        res_im = residue[1]

        def tabulate(t, carry):
            re, im, lre, lim = carry
            power_re[t] = re
            power_im[t] = im
            response[pl.ds(8 + t, 1)] = jnp.sum(lre, axis=0, keepdims=True)
            lre, lim = pole_re * lre - pole_im * lim, pole_re * lim + pole_im * lre
            lift_re[t] = lre
            lift_im[t] = lim
            return (pole_re * re - pole_im * im, pole_re * im + pole_im * re, lre, lim)

        one = jnp.ones((MODES, CH), F32)
        end_re, end_im, _, _ = lax.fori_loop(
            0, ROWS, tabulate, (one, jnp.zeros_like(one), res_re, res_im)
        )
        padded[pl.ds(0, ROWS)] = jnp.zeros((ROWS, CH), F32)
        response[pl.ds(0, 8)] = jnp.zeros((8, CH), F32)
        total[...] = jnp.zeros_like(total)
        shard_power[0] = end_re
        shard_power[1] = end_im

    def find_scale():
        small_here(p.along(-1), 3)
        small_here(p.along(1), 4)
        small_here(p.along(-3), 7)
        small_here(p.along(3), 8)
        small_here(p.along(4), 9)
        pl.semaphore_wait(hello.at[1], len(kin))
        summed = jnp.zeros((1, 128), F32)
        for z in range(Z):
            for j in range(4):
                summed = summed + stats[z, j, 0:1]
        scale_row = lax.rsqrt(summed / (FEATS * 4 * Z) + EPSILON)
        scales[...] = jnp.broadcast_to(scale_row, (ROWS, 128)).T
        for c in weight_loads:
            c.wait()

    def project(z):
        parts = []
        scale = scales[...]
        for j in range(4):
            x = wide[z, j // 2, j % 2].astype(F32)
            for h in range(2):
                part = x[:, 128 * h : 128 * h + 128] * scale * stats[z, j, 1 + h : 2 + h]
                parts.append(part.astype(BF16))
        normed = jnp.concatenate(parts, axis=1)
        rows = weight[pl.ds(pl.multiple_of(z * 4 * FEATS, 4 * FEATS), 4 * FEATS)]
        total[...] += jnp.dot(normed, rows, preferred_element_type=F32)

    spread = Gather(p, wide, tokens, WIDE_PLAN, send1, recv1)
    spread.run(
        project,
        {"stats1": stats1, "tables": tables, "stats2": stats2, "stats3": stats3, "scale": find_scale},
    )

    def close_spread():
        for c in small_sent:
            c.wait_send()
        spread.settle()

    projected = total[...].astype(BF16).astype(F32)
    ext[pl.ds(0, 8)] = jnp.zeros((8, 3 * CH), F32)
    ext[pl.ds(8, ROWS)] = projected
    convolved = []
    for i in range(3):
        lanes = pl.ds(i * CH, CH)
        c = jnp.zeros((ROWS, CH), F32)
        for lag in range(3):
            c = c + short_filter[lag, i : i + 1] * ext[pl.ds(8 - lag, ROWS), lanes]
        convolved.append(c)
    query, key, value = convolved
    row_of = lax.broadcasted_iota(jnp.int32, (ROWS, CH), 0)
    drive = jnp.where(row_of < 2, 0.0, key * value)
    padded[pl.ds(ROWS, ROWS)] = drive

    def gather_end(i, carry):
        out = []
        for j in range(4):
            re, im = carry[j]
            t = 4 * i + j
            u = padded[pl.ds(ROWS + t, 1)]
            out.append((re + power_re[ROWS - 1 - t] * u, im + power_im[ROWS - 1 - t] * u))
        return tuple(out)

    nothing = jnp.zeros((MODES, CH), F32)
    sums = lax.fori_loop(0, ROWS // 4, gather_end, ((nothing, nothing),) * 4)

    edges = [projected[ROWS - 2 :, i * CH : i * CH + CH] for i in range(3)]
    edges += [jnp.zeros((2, CH), F32), key[0:2], value[0:2], jnp.zeros((4, CH), F32)]
    ends[p.seq, pl.ds(0, MODES)] = sums[0][0] + sums[1][0] + sums[2][0] + sums[3][0]
    ends[p.seq, pl.ds(MODES, MODES)] = sums[0][1] + sums[1][1] + sums[2][1] + sums[3][1]
    ends[p.seq, pl.ds(2 * MODES, 16)] = jnp.concatenate(edges, axis=0)
    here = ends.at[p.seq]

    def end_copy(i):
        return small(here, here, 10 + i, ((p.seq + i) % SEQ, p.chan))

    for i in (6, 5, 7, 4, 2, 3, 1):

        @pl.when(p.seq + i < SEQ)
        def _():
            end_copy(i).start()

    def close_state():
        for i in range(1, SEQ):

            @pl.when(p.seq + i < SEQ)
            def _():
                end_copy(i).wait_send()

    def respond(i, acc):
        for j in range(4):
            lag = 4 * i + j
            acc = acc + response[pl.ds(8 + lag, 1)] * padded[pl.ds(ROWS - lag, ROWS)]
        return acc

    mode_out = lax.fori_loop(0, ROWS // 4, respond, jnp.zeros((ROWS, CH), F32))
    close_spread()

    def first_rows(i, so_far):
        near, far = short_filter[1, i : i + 1], short_filter[2, i : i + 1]
        before = rim[pl.ds(2 * i, 2)]
        return (
            so_far[0:1] + near * before[1:2] + far * before[0:1],
            so_far[1:2] + far * before[1:2],
        )

    def first_drive(key_rows, value_rows):
        (key0, key1), (value0, value1) = first_rows(1, key_rows), first_rows(2, value_rows)
        return key0 * value0, key1 * value1

    for i in range(3):
        rim[pl.ds(2 * i, 2)] = prior_rows[i].astype(F32)
    shard_re, shard_im = shard_power[0], shard_power[1]
    last_re, last_im = power_re[ROWS - 1], power_im[ROWS - 1]
    next_re, next_im = power_re[ROWS - 2], power_im[ROWS - 2]
    for j in range(SEQ - 1):

        @pl.when(j < p.seq)
        def _():
            theirs = ends.at[j]
            for i in range(1, SEQ):

                @pl.when(p.seq - j == i)
                def _():
                    small(theirs, theirs, 10 + i, (j, p.chan)).wait_recv()

            drive0, drive1 = first_drive(ends[j, pl.ds(40, 2)], ends[j, pl.ds(42, 2)])
            re, im = incoming[0], incoming[1]
            end_re = ends[j, pl.ds(0, MODES)] + last_re * drive0 + next_re * drive1
            end_im = ends[j, pl.ds(MODES, MODES)] + last_im * drive0 + next_im * drive1
            incoming[0] = shard_re * re - shard_im * im + end_re
            incoming[1] = shard_re * im + shard_im * re + end_im
            rim[pl.ds(0, 6)] = ends[j, pl.ds(32, 6)]

    in_re, in_im = incoming[0], incoming[1]
    carried = []
    for b in range(ROWS // 8):
        lre = lift_re[pl.ds(8 * b, 8)]
        lim = lift_im[pl.ds(8 * b, 8)]
        carried.append(jnp.sum(lre * in_re[None] - lim * in_im[None], axis=1))
    drive0, drive1 = first_drive(key[0:2], value[0:2])
    query0, query1 = first_rows(0, query[0:2])
    first, second = row_of == 0, row_of == 1
    drive = jnp.where(first, drive0, jnp.where(second, drive1, drive))
    query = jnp.where(first, query0, jnp.where(second, query1, query))
    mode_out = mode_out + response[pl.ds(8, ROWS)] * drive0 + response[pl.ds(7, ROWS)] * drive1
    mode_out = mode_out + jnp.concatenate(carried, axis=0)
    narrow[p.z, p.y, p.k] = (query * (mode_out + skip_weight[...] * drive)).astype(BF16)

    total[:, pl.ds(0, FEATS)] = own[...].astype(F32)
    last_load.wait()

    def output(z):
        parts = [narrow[z, j // 2, j % 2] for j in range(4)]
        rows = last_weight[pl.ds(pl.multiple_of(z * 4 * CH, 4 * CH), 4 * CH)]
        total[:, pl.ds(0, FEATS)] += jnp.dot(
            jnp.concatenate(parts, axis=1), rows, preferred_element_type=F32
        )

    mix = Gather(p, narrow, None, NARROW_PLAN, send2, recv2)

    def settle():
        if not mix.settled:
            close_state()
        mix.settle(in_flight=8)

    mix.run(output, {"settle": settle})
    mixed[...] = total[:, pl.ds(0, FEATS)].astype(BF16)

    mix.settle()


def body(
    tokens,
    norm_gain,
    in_weight,
    short_filter,
    prior_rows,
    decay_rate,
    pole_angle,
    residue,
    prior_state,
    skip_weight,
    out_weight,
):
    vmem = pl.BlockSpec(memory_space=pltpu.VMEM)
    hbm = pl.BlockSpec(memory_space=pltpu.HBM)
    flops = 2 * ROWS * (FEATS * 32 * 3 * CH + CH * 32 * FEATS)
    return pl.pallas_call(
        kernel,
        out_shape=jax.ShapeDtypeStruct((ROWS, FEATS), BF16),
        in_specs=[hbm] * 11,
        out_specs=vmem,
        scratch_shapes=[
            pltpu.VMEM((FEATS,), BF16),
            pltpu.VMEM((3, 3, CH), F32),
            pltpu.VMEM((3, 2, CH), BF16),
            pltpu.VMEM((MODES, CH), F32),
            pltpu.VMEM((MODES, CH), F32),
            pltpu.VMEM((2, MODES, CH), F32),
            pltpu.VMEM((1, CH), F32),
            pltpu.VMEM((ROWS, FEATS), BF16),
            pltpu.VMEM((Z, 2, 2, ROWS, FEATS), BF16),
            pltpu.VMEM((Z, 4, 8, 128), F32),
            pltpu.VMEM((Z * 4 * FEATS, 3 * CH), BF16),
            pltpu.VMEM((Z, 2, 2, ROWS, CH), BF16),
            pltpu.VMEM((Z * 4 * CH, FEATS), BF16),
            pltpu.VMEM((ROWS, MODES, CH), F32),
            pltpu.VMEM((ROWS, MODES, CH), F32),
            pltpu.VMEM((ROWS, MODES, CH), F32),
            pltpu.VMEM((ROWS, MODES, CH), F32),
            pltpu.VMEM((8 + ROWS, CH), F32),
            pltpu.VMEM((ROWS, 3 * CH), F32),
            pltpu.VMEM((8, CH), F32),
            pltpu.VMEM((8 + ROWS, 3 * CH), F32),
            pltpu.VMEM((2 * ROWS, CH), F32),
            pltpu.VMEM((SEQ, 2 * MODES + 16, CH), F32),
            pltpu.VMEM((2, MODES, CH), F32),
            pltpu.VMEM((2, MODES, CH), F32),
            pltpu.VMEM((ROWS, 128), F32),
            pltpu.SemaphoreType.REGULAR((2,)),
            pltpu.SemaphoreType.DMA((13,)),
            pltpu.SemaphoreType.DMA((len(WIDE_PLAN),)),
            pltpu.SemaphoreType.DMA((len(WIDE_PLAN),)),
            pltpu.SemaphoreType.DMA((len(NARROW_PLAN),)),
            pltpu.SemaphoreType.DMA((len(NARROW_PLAN),)),
            pltpu.SemaphoreType.DMA((18,)),
            pltpu.SemaphoreType.DMA((18,)),
        ],
        compiler_params=pltpu.CompilerParams(
            collective_id=0, has_side_effects=True, vmem_limit_bytes=60 * 1024 * 1024
        ),
        cost_estimate=pl.CostEstimate(flops=flops, bytes_accessed=9 * 1024 * 1024, transcendentals=0),
    )(
        tokens,
        norm_gain,
        jnp.transpose(in_weight, (1, 0, 2)),
        short_filter,
        jnp.transpose(prior_rows, (1, 0, 2)),
        decay_rate.T,
        pole_angle.T,
        jnp.transpose(residue, (0, 2, 1)),
        jnp.transpose(prior_state, (0, 2, 1)),
        skip_weight.reshape(1, CH),
        out_weight,
    )


def solution(mesh):
    return jax.shard_map(
        body,
        mesh=mesh,
        in_specs=(
            P("seq", "chan"),
            P("chan"),
            P(None, None, "chan"),
            P(None, None, "chan"),
            P(None, None, "chan"),
            P("chan", None),
            P("chan", None),
            P(None, "chan", None),
            P(None, "chan", None),
            P("chan"),
            P(None, "chan"),
        ),
        out_specs=P("seq", "chan"),
        check_vma=False,
    )
```

```python
import jax
import jax.numpy as jnp
from jax import lax
from jax.experimental import pallas as pl
from jax.experimental.pallas import tpu as pltpu
from jax.sharding import PartitionSpec as P

MESH = pl.DeviceIdType.MESH
EPSILON = 1e-06
F32 = jnp.float32
BF16 = jnp.bfloat16

Z = 8
ROWS = 128
FEATS = 256
CH = 128
MODES = 16
SEQ = 8


class Place:
    def __init__(self):
        self.seq = lax.axis_index("seq")
        chan = lax.axis_index("chan")
        self.chan = chan
        self.z = chan // 4
        self.y = (chan // 2) % 2
        self.k = chan % 2

    def at(self, z, y, k):
        return (self.seq, z * 4 + y * 2 + k)

    def to(self, dz, dy, dk):
        return self.at(self.along(dz), (self.y + dy) % 2, (self.k + dk) % 2)

    def along(self, by):
        return (self.z + by + Z) % Z


WIDE_PLAN = (
    (0, 0, 0, 128, 2, 0, 0),
    (0, 0, 0, 128, -2, 0, 0),
    (0, 0, 0, 128, 1, 0, 0),
    (0, 0, 0, 128, -1, 0, 0),
    (0, 0, 0, 128, 0, 1, 0),
    (0, 0, 0, 128, 0, 0, 1),
    "stats1",
    "tables",
    (0, 1, 64, 64, 2, 0, 0),
    (0, 1, 64, 64, -2, 0, 0),
    (0, 1, 0, 128, 0, 0, 1),
    (-2, 0, 32, 32, 2, 0, 0),
    (2, 0, 0, 32, -2, 0, 0),
    (-2, 0, 96, 32, 2, 0, 0),
    (-2, 0, 0, 96, 1, 0, 0),
    (2, 0, 0, 96, -1, 0, 0),
    (-2, 0, 0, 64, 0, 1, 0),
    (2, 0, 0, 64, 0, 1, 0),
    (-2, 0, 0, 128, 0, 0, 1),
    (2, 0, 0, 128, 0, 0, 1),
    (-1, 0, 96, 32, 2, 0, 0),
    (1, 0, 64, 32, -3, 0, 0),
    (1, 0, 96, 32, -2, 0, 0),
    (-1, 0, 0, 128, 0, 1, 0),
    "stats2",
    "stats3",
    (1, 0, 0, 128, 0, 1, 0),
    (-1, 0, 0, 128, 0, 0, 1),
    (1, 0, 0, 128, 0, 0, 1),
    (-2, 1, 96, 32, 2, 0, 0),
    (2, 1, 64, 32, -2, 0, 0),
    (-2, 1, 0, 128, 1, 0, 0),
    (-2, 1, 0, 128, 0, 0, 1),
    (4, 0, 0, 64, 0, 1, 0),
    (2, 1, 32, 96, -1, 0, 0),
    (2, 1, 0, 128, 0, 0, 1),
    (3, 0, 0, 32, 0, 1, 0),
    (-1, 1, 0, 128, 0, 0, 1),
    (-3, 0, 0, 128, 0, 0, 1),
    (4, 0, 0, 128, 0, 0, 1),
    (3, 0, 0, 128, 0, 0, 1),
    (1, 1, 0, 128, 0, 0, 1),
    (4, 1, 0, 128, 0, 0, 1),
    (-3, 1, 0, 128, 0, 0, 1),
    (3, 1, 0, 128, 0, 0, 1),
    "scale",
    0,
    -2,
    2,
    -1,
    1,
    4,
    -3,
    3,
)

NARROW_PLAN = (
    (0, 0, 0, 128, 3, 0, 0),
    (0, 0, 0, 128, -3, 0, 0),
    (0, 0, 0, 128, 2, 0, 0),
    (0, 0, 0, 128, -2, 0, 0),
    (0, 0, 0, 128, 1, 0, 0),
    (0, 0, 0, 128, -1, 0, 0),
    (0, 0, 0, 128, 0, 1, 0),
    (0, 0, 0, 128, 0, 0, 1),
    (0, 1, 0, 128, 4, 0, 0),
    (0, 1, 0, 128, -2, 0, 0),
    (0, 1, 0, 128, 1, 0, 0),
    (0, 1, 0, 128, -1, 0, 0),
    (0, 1, 0, 128, 0, 0, 1),
    0,
    (-3, 0, 0, 128, 0, 1, 0),
    (3, 0, 0, 128, -1, 0, 0),
    (3, 0, 0, 128, 0, 1, 0),
    (-3, 0, 0, 128, 0, 0, 1),
    (3, 0, 0, 128, 0, 0, 1),
    (-2, 0, 0, 128, 0, 1, 0),
    (-2, 0, 0, 128, 0, 0, 1),
    (2, 0, 0, 128, 0, 0, 1),
    (-1, 0, 0, 128, 0, 0, 1),
    (1, 0, 0, 128, 0, 0, 1),
    "settle",
    (2, 1, 0, 128, 0, 0, 1),
    (-3, 1, 0, 128, 0, 0, 1),
    (1, 1, 0, 128, 0, 0, 1),
    (3, 1, 0, 128, 0, 0, 1),
    (4, 0, 0, 128, 0, 0, 1),
    2,
    "settle",
    (-1, 1, 0, 128, 0, 0, 1),
    (-2, 1, 0, 128, 0, 0, 1),
    -3,
    1,
    (4, 1, 0, 128, 0, 0, 1),
    3,
    -1,
    -2,
    4,
)


def nearest(dz):
    dz %= Z
    return dz - Z if dz > Z // 2 else dz


class Gather:
    def __init__(self, place, buf, own, plan, send_sem, recv_sem):
        self.p, self.buf, self.own, self.plan = place, buf, own, plan
        self.send_sem, self.recv_sem = send_sem, recv_sem
        self.sends = [step for step in plan if isinstance(step, tuple)]
        self.brings = {}
        for i, (dz, dy, first, rows, tz, ty, tk) in enumerate(self.sends):
            for r in range(first, first + rows, 16):
                self.brings[nearest(dz - tz), dy ^ ty, tk, r] = i
        self.waited = set()
        self.sent = []
        self.settled = 0

    def copy(self, i, block, device):
        p = self.p
        dz, dy, dk = block
        first, rows = self.sends[i][2:4]
        here = self.buf.at[p.along(dz), (p.y + dy) % 2, (p.k + dk) % 2, pl.ds(first, rows)]
        mine = self.own is not None and block == (0, 0, 0)
        return pltpu.make_async_remote_copy(
            src_ref=self.own.at[pl.ds(first, rows)] if mine else here,
            dst_ref=here,
            send_sem=self.send_sem.at[i],
            recv_sem=self.recv_sem.at[i],
            device_id=device,
            device_id_type=MESH,
        )

    def need(self, block, first, rows):
        if block == (0, 0, 0):
            return
        for r in range(first, first + rows, 16):
            i = self.brings[block + (r,)]
            if i not in self.waited:
                self.waited.add(i)
                dz, dy, _, _, tz, ty, tk = self.sends[i]
                self.copy(i, (nearest(dz - tz), dy ^ ty, tk), self.p.to(0, 0, 1)).wait_recv()

    def run(self, on_chip, named):
        for step in self.plan:
            if isinstance(step, str):
                named[step]()
            elif isinstance(step, int):
                for block in ((step, 0, 0), (step, 1, 0), (step, 0, 1), (step, 1, 1)):
                    self.need(block, 0, ROWS)
                on_chip(self.p.along(step))
            else:
                dz, dy, first, rows, tz, ty, tk = step
                self.need((nearest(dz), dy, 0), first, rows)
                c = self.copy(len(self.sent), (dz, dy, 0), self.p.to(tz, ty, tk))
                c.start()
                self.sent.append(c)

    def settle(self, in_flight=0):
        upto = max(self.settled, len(self.sent) - in_flight)
        for c in self.sent[self.settled : upto]:
            c.wait_send()
        self.settled = upto


def kernel(
    tokens,
    gain_hbm,
    in_weight,
    filter_hbm,
    rows_hbm,
    decay_hbm,
    angle_hbm,
    residue_hbm,
    state_hbm,
    skip_hbm,
    out_weight,
    mixed,
    gain,
    short_filter,
    prior_rows,
    decay_rate,
    pole_angle,
    residue,
    skip_weight,
    own,
    wide,
    stats,
    weight,
    narrow,
    last_weight,
    power_re,
    power_im,
    lift_re,
    lift_im,
    response,
    total,
    rim,
    ext,
    padded,
    ends,
    incoming,
    shard_power,
    scales,
    hello,
    local_sem,
    send1,
    recv1,
    send2,
    recv2,
    small_send,
    small_recv,
):
    p = Place()
    barrier = pltpu.get_barrier_semaphore()
    kin = [
        (4 * (p.seq // 4) + (p.seq + 1) % 4, p.chan),
        (4 * (p.seq // 4) + (p.seq + 3) % 4, p.chan),
        ((p.seq + 4) % SEQ, p.chan),
    ]
    greeted = [p.to(*by) for by in ((0, 0, 1), (0, 1, 0), (0, 1, 1), (1, 0, 0), (-1, 0, 0), (2, 0, 0), (-2, 0, 0))]
    greeted += kin
    for device in greeted:
        pl.semaphore_signal(barrier, inc=1, device_id=device, device_id_type=MESH)

    pairs = (
        (tokens, own),
        (gain_hbm, gain),
        (filter_hbm, short_filter),
        (rows_hbm, prior_rows),
        (decay_hbm, decay_rate),
        (angle_hbm, pole_angle),
        (residue_hbm, residue),
        (state_hbm, incoming),
        (skip_hbm, skip_weight),
    )
    loads = [pltpu.make_async_copy(a, b, local_sem.at[4 + i]) for i, (a, b) in enumerate(pairs)]
    weight_loads = []
    for i in range(3):
        weight_loads.append(
            pltpu.make_async_copy(in_weight.at[i], weight.at[:, pl.ds(i * CH, CH)], local_sem.at[i])
        )
    last_load = pltpu.make_async_copy(out_weight, last_weight, local_sem.at[3])
    for c in loads + weight_loads + [last_load]:
        c.start()

    pl.semaphore_wait(barrier, len(greeted))

    def small(src, dst, index, device):
        return pltpu.make_async_remote_copy(
            src_ref=src,
            dst_ref=dst,
            send_sem=small_send.at[index],
            recv_sem=small_recv.at[index],
            device_id=device,
            device_id_type=MESH,
        )

    small_sent = []

    def spread_small(src, index, device):
        c = small(src, src, index, device)
        c.start()
        small_sent.append(c)

    def small_here(z, index):
        small(stats.at[z], stats.at[z], index, p.to(0, 0, 1)).wait_recv()

    pair = ((0, 1), (1, 0), (1, 1))

    def stats1():
        loads[0].wait()
        loads[1].wait()
        values = own[...].astype(F32)
        squares = jnp.sum(values * values, axis=1, keepdims=True)
        row = jnp.broadcast_to(squares, (ROWS, 128)).T
        gains = gain[...].astype(F32).reshape(1, FEATS)
        stats[p.z, 2 * p.y + p.k] = jnp.concatenate(
            [row[0:1], gains[:, 0:128], gains[:, 128:256], row[3:4]], axis=0
        )
        wide[p.z, p.y, p.k] = own[...]
        for i, (dy, dk) in enumerate(pair):
            spread_small(stats.at[p.z, 2 * p.y + p.k], i, p.to(0, dy, dk))
        for device in kin:
            pl.semaphore_signal(hello.at[0], inc=1, device_id=device, device_id_type=MESH)

    def stats2():
        for i, (dy, dk) in enumerate(pair):
            theirs = stats.at[p.z, 2 * ((p.y + dy) % 2) + (p.k + dk) % 2]
            small(theirs, theirs, i, p.to(0, dy, dk)).wait_recv()
        for i, by in enumerate((1, -1, 2, -2)):
            spread_small(stats.at[p.z], 3 + i, p.to(by, 0, 0))

    def stats3():
        for i, by in enumerate((3, -3, 4)):
            spread_small(stats.at[p.z], 7 + i, p.to(by, 0, 0))

    def tables():
        for c in loads[2:]:
            c.wait()
        magnitude = jnp.exp(-decay_rate[...])
        pole_re = magnitude * jnp.cos(pole_angle[...])
        pole_im = magnitude * jnp.sin(pole_angle[...])
        res_re = residue[0]
        res_im = residue[1]

        def tabulate(t, carry):
            re, im, lre, lim = carry
            power_re[t] = re
            power_im[t] = im
            response[pl.ds(8 + t, 1)] = jnp.sum(lre, axis=0, keepdims=True)
            lre, lim = pole_re * lre - pole_im * lim, pole_re * lim + pole_im * lre
            lift_re[t] = lre
            lift_im[t] = lim
            return (pole_re * re - pole_im * im, pole_re * im + pole_im * re, lre, lim)

        one = jnp.ones((MODES, CH), F32)
        end_re, end_im, _, _ = lax.fori_loop(
            0, ROWS, tabulate, (one, jnp.zeros_like(one), res_re, res_im)
        )
        padded[pl.ds(0, ROWS)] = jnp.zeros((ROWS, CH), F32)
        response[pl.ds(0, 8)] = jnp.zeros((8, CH), F32)
        total[...] = jnp.zeros_like(total)
        shard_power[0] = end_re
        shard_power[1] = end_im

    def find_scale():
        for i, by in enumerate((1, -1, 2, -2, 3, -3, 4)):
            small_here(p.along(-by), 3 + i)
        pl.semaphore_wait(hello.at[0], len(kin))
        for device in kin:
            pl.semaphore_signal(hello.at[1], inc=1, device_id=device, device_id_type=MESH)
        summed = jnp.zeros((1, 128), F32)
        for z in range(Z):
            for j in range(4):
                summed = summed + stats[z, j, 0:1]
        scale_row = lax.rsqrt(summed / (FEATS * 4 * Z) + EPSILON)
        scales[...] = jnp.broadcast_to(scale_row, (ROWS, 128)).T
        for c in weight_loads:
            c.wait()

    def project(z):
        parts = []
        scale = scales[...]
        for j in range(4):
            x = wide[z, j // 2, j % 2].astype(F32)
            for h in range(2):
                part = x[:, 128 * h : 128 * h + 128] * scale * stats[z, j, 1 + h : 2 + h]
                parts.append(part.astype(BF16))
        normed = jnp.concatenate(parts, axis=1)
        rows = weight[pl.ds(pl.multiple_of(z * 4 * FEATS, 4 * FEATS), 4 * FEATS)]
        total[...] += jnp.dot(normed, rows, preferred_element_type=F32)

    spread = Gather(p, wide, tokens, WIDE_PLAN, send1, recv1)
    spread.run(
        project,
        {"stats1": stats1, "tables": tables, "stats2": stats2, "stats3": stats3, "scale": find_scale},
    )

    def close_spread():
        for c in small_sent:
            c.wait_send()
        spread.settle()

    projected = total[...].astype(BF16).astype(F32)
    ext[pl.ds(0, 8)] = jnp.zeros((8, 3 * CH), F32)
    ext[pl.ds(8, ROWS)] = projected
    convolved = []
    for i in range(3):
        lanes = pl.ds(i * CH, CH)
        c = jnp.zeros((ROWS, CH), F32)
        for lag in range(3):
            c = c + short_filter[lag, i : i + 1] * ext[pl.ds(8 - lag, ROWS), lanes]
        convolved.append(c)
    query, key, value = convolved
    row_of = lax.broadcasted_iota(jnp.int32, (ROWS, CH), 0)
    drive = jnp.where(row_of < 2, 0.0, key * value)
    padded[pl.ds(ROWS, ROWS)] = drive

    def gather_end(i, carry):
        out = []
        for j in range(4):
            re, im = carry[j]
            t = 4 * i + j
            u = padded[pl.ds(ROWS + t, 1)]
            out.append((re + power_re[ROWS - 1 - t] * u, im + power_im[ROWS - 1 - t] * u))
        return tuple(out)

    nothing = jnp.zeros((MODES, CH), F32)
    sums = lax.fori_loop(0, ROWS // 4, gather_end, ((nothing, nothing),) * 4)

    edges = [projected[ROWS - 2 :, i * CH : i * CH + CH] for i in range(3)]
    edges += [jnp.zeros((2, CH), F32), key[0:2], value[0:2], jnp.zeros((4, CH), F32)]
    ends[p.seq, pl.ds(0, MODES)] = sums[0][0] + sums[1][0] + sums[2][0] + sums[3][0]
    ends[p.seq, pl.ds(MODES, MODES)] = sums[0][1] + sums[1][1] + sums[2][1] + sums[3][1]
    ends[p.seq, pl.ds(2 * MODES, 16)] = jnp.concatenate(edges, axis=0)
    here = ends.at[p.seq]

    def end_copy(i):
        return small(here, here, 10 + i, ((p.seq + i) % SEQ, p.chan))

    pl.semaphore_wait(hello.at[1], len(kin))
    for i in (6, 5, 7, 4, 2, 3, 1):

        @pl.when(p.seq + i < SEQ)
        def _():
            end_copy(i).start()

    def close_state():
        for i in range(1, SEQ):

            @pl.when(p.seq + i < SEQ)
            def _():
                end_copy(i).wait_send()

    def respond(i, acc):
        for j in range(4):
            lag = 4 * i + j
            acc = acc + response[pl.ds(8 + lag, 1)] * padded[pl.ds(ROWS - lag, ROWS)]
        return acc

    mode_out = lax.fori_loop(0, ROWS // 4, respond, jnp.zeros((ROWS, CH), F32))
    close_spread()

    def first_rows(i, so_far):
        near, far = short_filter[1, i : i + 1], short_filter[2, i : i + 1]
        before = rim[pl.ds(2 * i, 2)]
        return (
            so_far[0:1] + near * before[1:2] + far * before[0:1],
            so_far[1:2] + far * before[1:2],
        )

    def first_drive(key_rows, value_rows):
        (key0, key1), (value0, value1) = first_rows(1, key_rows), first_rows(2, value_rows)
        return key0 * value0, key1 * value1

    for i in range(3):
        rim[pl.ds(2 * i, 2)] = prior_rows[i].astype(F32)
    shard_re, shard_im = shard_power[0], shard_power[1]
    last_re, last_im = power_re[ROWS - 1], power_im[ROWS - 1]
    next_re, next_im = power_re[ROWS - 2], power_im[ROWS - 2]
    for j in range(SEQ - 1):

        @pl.when(j < p.seq)
        def _():
            theirs = ends.at[j]
            for i in range(1, SEQ):

                @pl.when(p.seq - j == i)
                def _():
                    small(theirs, theirs, 10 + i, (j, p.chan)).wait_recv()

            drive0, drive1 = first_drive(ends[j, pl.ds(40, 2)], ends[j, pl.ds(42, 2)])
            re, im = incoming[0], incoming[1]
            end_re = ends[j, pl.ds(0, MODES)] + last_re * drive0 + next_re * drive1
            end_im = ends[j, pl.ds(MODES, MODES)] + last_im * drive0 + next_im * drive1
            incoming[0] = shard_re * re - shard_im * im + end_re
            incoming[1] = shard_re * im + shard_im * re + end_im
            rim[pl.ds(0, 6)] = ends[j, pl.ds(32, 6)]

    in_re, in_im = incoming[0], incoming[1]
    carried = []
    for b in range(ROWS // 8):
        lre = lift_re[pl.ds(8 * b, 8)]
        lim = lift_im[pl.ds(8 * b, 8)]
        carried.append(jnp.sum(lre * in_re[None] - lim * in_im[None], axis=1))
    drive0, drive1 = first_drive(key[0:2], value[0:2])
    query0, query1 = first_rows(0, query[0:2])
    first, second = row_of == 0, row_of == 1
    drive = jnp.where(first, drive0, jnp.where(second, drive1, drive))
    query = jnp.where(first, query0, jnp.where(second, query1, query))
    mode_out = mode_out + response[pl.ds(8, ROWS)] * drive0 + response[pl.ds(7, ROWS)] * drive1
    mode_out = mode_out + jnp.concatenate(carried, axis=0)
    narrow[p.z, p.y, p.k] = (query * (mode_out + skip_weight[...] * drive)).astype(BF16)

    total[:, pl.ds(0, FEATS)] = own[...].astype(F32)
    last_load.wait()

    def output(z):
        parts = [narrow[z, j // 2, j % 2] for j in range(4)]
        rows = last_weight[pl.ds(pl.multiple_of(z * 4 * CH, 4 * CH), 4 * CH)]
        total[:, pl.ds(0, FEATS)] += jnp.dot(
            jnp.concatenate(parts, axis=1), rows, preferred_element_type=F32
        )

    mix = Gather(p, narrow, None, NARROW_PLAN, send2, recv2)

    def settle():
        if not mix.settled:
            close_state()
        mix.settle(in_flight=8)

    mix.run(output, {"settle": settle})
    mixed[...] = total[:, pl.ds(0, FEATS)].astype(BF16)

    mix.settle()


def body(
    tokens,
    norm_gain,
    in_weight,
    short_filter,
    prior_rows,
    decay_rate,
    pole_angle,
    residue,
    prior_state,
    skip_weight,
    out_weight,
):
    vmem = pl.BlockSpec(memory_space=pltpu.VMEM)
    hbm = pl.BlockSpec(memory_space=pltpu.HBM)
    flops = 2 * ROWS * (FEATS * 32 * 3 * CH + CH * 32 * FEATS)
    return pl.pallas_call(
        kernel,
        out_shape=jax.ShapeDtypeStruct((ROWS, FEATS), BF16),
        in_specs=[hbm] * 11,
        out_specs=vmem,
        scratch_shapes=[
            pltpu.VMEM((FEATS,), BF16),
            pltpu.VMEM((3, 3, CH), F32),
            pltpu.VMEM((3, 2, CH), BF16),
            pltpu.VMEM((MODES, CH), F32),
            pltpu.VMEM((MODES, CH), F32),
            pltpu.VMEM((2, MODES, CH), F32),
            pltpu.VMEM((1, CH), F32),
            pltpu.VMEM((ROWS, FEATS), BF16),
            pltpu.VMEM((Z, 2, 2, ROWS, FEATS), BF16),
            pltpu.VMEM((Z, 4, 4, 128), F32),
            pltpu.VMEM((Z * 4 * FEATS, 3 * CH), BF16),
            pltpu.VMEM((Z, 2, 2, ROWS, CH), BF16),
            pltpu.VMEM((Z * 4 * CH, FEATS), BF16),
            pltpu.VMEM((ROWS, MODES, CH), F32),
            pltpu.VMEM((ROWS, MODES, CH), F32),
            pltpu.VMEM((ROWS, MODES, CH), F32),
            pltpu.VMEM((ROWS, MODES, CH), F32),
            pltpu.VMEM((8 + ROWS, CH), F32),
            pltpu.VMEM((ROWS, 3 * CH), F32),
            pltpu.VMEM((8, CH), F32),
            pltpu.VMEM((8 + ROWS, 3 * CH), F32),
            pltpu.VMEM((2 * ROWS, CH), F32),
            pltpu.VMEM((SEQ, 2 * MODES + 16, CH), F32),
            pltpu.VMEM((2, MODES, CH), F32),
            pltpu.VMEM((2, MODES, CH), F32),
            pltpu.VMEM((ROWS, 128), F32),
            pltpu.SemaphoreType.REGULAR((2,)),
            pltpu.SemaphoreType.DMA((13,)),
            pltpu.SemaphoreType.DMA((len(WIDE_PLAN),)),
            pltpu.SemaphoreType.DMA((len(WIDE_PLAN),)),
            pltpu.SemaphoreType.DMA((len(NARROW_PLAN),)),
            pltpu.SemaphoreType.DMA((len(NARROW_PLAN),)),
            pltpu.SemaphoreType.DMA((18,)),
            pltpu.SemaphoreType.DMA((18,)),
        ],
        compiler_params=pltpu.CompilerParams(
            collective_id=0, has_side_effects=True, vmem_limit_bytes=60 * 1024 * 1024
        ),
        cost_estimate=pl.CostEstimate(flops=flops, bytes_accessed=9 * 1024 * 1024, transcendentals=0),
    )(
        tokens,
        norm_gain,
        jnp.transpose(in_weight, (1, 0, 2)),
        short_filter,
        jnp.transpose(prior_rows, (1, 0, 2)),
        decay_rate.T,
        pole_angle.T,
        jnp.transpose(residue, (0, 2, 1)),
        jnp.transpose(prior_state, (0, 2, 1)),
        skip_weight.reshape(1, CH),
        out_weight,
    )


def solution(mesh):
    return jax.shard_map(
        body,
        mesh=mesh,
        in_specs=(
            P("seq", "chan"),
            P("chan"),
            P(None, None, "chan"),
            P(None, None, "chan"),
            P(None, None, "chan"),
            P("chan", None),
            P("chan", None),
            P(None, "chan", None),
            P(None, "chan", None),
            P("chan"),
            P(None, "chan"),
        ),
        out_specs=P("seq", "chan"),
        check_vma=False,
    )
```

```python
import jax
import jax.numpy as jnp
from jax import lax
from jax.experimental import pallas as pl
from jax.experimental.pallas import tpu as pltpu
from jax.sharding import PartitionSpec as P

MESH = pl.DeviceIdType.MESH
EPSILON = 1e-06
F32 = jnp.float32
BF16 = jnp.bfloat16

Z = 8
ROWS = 128
FEATS = 256
CH = 128
MODES = 16
SEQ = 8


class Place:
    def __init__(self):
        self.seq = lax.axis_index("seq")
        chan = lax.axis_index("chan")
        self.chan = chan
        self.z = chan // 4
        self.y = (chan // 2) % 2
        self.k = chan % 2

    def at(self, z, y, k):
        return (self.seq, z * 4 + y * 2 + k)

    def to(self, dz, dy, dk):
        return self.at(self.along(dz), (self.y + dy) % 2, (self.k + dk) % 2)

    def along(self, by):
        return (self.z + by + Z) % Z


WIDE_PLAN = (
    (0, 0, 0, 128, 2, 0, 0),
    (0, 0, 0, 128, -2, 0, 0),
    (0, 0, 0, 128, 1, 0, 0),
    (0, 0, 0, 128, -1, 0, 0),
    (0, 0, 0, 128, 0, 1, 0),
    (0, 0, 0, 128, 0, 0, 1),
    "stats1",
    "tables",
    (0, 1, 64, 64, 2, 0, 0),
    (0, 1, 64, 64, -2, 0, 0),
    (0, 1, 0, 128, 0, 0, 1),
    (-2, 0, 32, 32, 2, 0, 0),
    (2, 0, 0, 32, -2, 0, 0),
    (-2, 0, 96, 32, 2, 0, 0),
    (-2, 0, 0, 96, 1, 0, 0),
    (2, 0, 0, 96, -1, 0, 0),
    (-2, 0, 0, 64, 0, 1, 0),
    (2, 0, 0, 64, 0, 1, 0),
    (-2, 0, 0, 128, 0, 0, 1),
    (2, 0, 0, 128, 0, 0, 1),
    (-1, 0, 96, 32, 2, 0, 0),
    (1, 0, 64, 32, -3, 0, 0),
    (1, 0, 96, 32, -2, 0, 0),
    (-1, 0, 0, 128, 0, 1, 0),
    "stats2",
    "stats3",
    (1, 0, 0, 128, 0, 1, 0),
    (-1, 0, 0, 128, 0, 0, 1),
    (1, 0, 0, 128, 0, 0, 1),
    (-2, 1, 96, 32, 2, 0, 0),
    (2, 1, 64, 32, -2, 0, 0),
    (-2, 1, 0, 128, 1, 0, 0),
    (-2, 1, 0, 128, 0, 0, 1),
    (4, 0, 0, 64, 0, 1, 0),
    (2, 1, 32, 96, -1, 0, 0),
    (2, 1, 0, 128, 0, 0, 1),
    (3, 0, 0, 32, 0, 1, 0),
    (-1, 1, 0, 128, 0, 0, 1),
    (-3, 0, 0, 128, 0, 0, 1),
    (4, 0, 0, 128, 0, 0, 1),
    (3, 0, 0, 128, 0, 0, 1),
    (1, 1, 0, 128, 0, 0, 1),
    (4, 1, 0, 128, 0, 0, 1),
    (-3, 1, 0, 128, 0, 0, 1),
    (3, 1, 0, 128, 0, 0, 1),
    "scale",
    0,
    -2,
    2,
    -1,
    1,
    4,
    -3,
    3,
)

NARROW_PLAN = (
    (0, 0, 0, 128, 3, 0, 0),
    (0, 0, 0, 128, -3, 0, 0),
    (0, 0, 0, 128, 2, 0, 0),
    (0, 0, 0, 128, -2, 0, 0),
    (0, 0, 0, 128, 1, 0, 0),
    (0, 0, 0, 128, -1, 0, 0),
    (0, 0, 0, 128, 0, 1, 0),
    (0, 0, 0, 128, 0, 0, 1),
    "begin",
    (0, 1, 0, 128, 4, 0, 0),
    (0, 1, 0, 128, -2, 0, 0),
    (0, 1, 0, 128, 1, 0, 0),
    (0, 1, 0, 128, -1, 0, 0),
    (0, 1, 0, 128, 0, 0, 1),
    0,
    (-3, 0, 0, 128, 0, 1, 0),
    (3, 0, 0, 128, -1, 0, 0),
    (3, 0, 0, 128, 0, 1, 0),
    (-3, 0, 0, 128, 0, 0, 1),
    (3, 0, 0, 128, 0, 0, 1),
    (-2, 0, 0, 128, 0, 1, 0),
    (-2, 0, 0, 128, 0, 0, 1),
    (2, 0, 0, 128, 0, 0, 1),
    (-1, 0, 0, 128, 0, 0, 1),
    (1, 0, 0, 128, 0, 0, 1),
    "settle",
    (2, 1, 0, 128, 0, 0, 1),
    (-3, 1, 0, 128, 0, 0, 1),
    (1, 1, 0, 128, 0, 0, 1),
    (3, 1, 0, 128, 0, 0, 1),
    (4, 0, 0, 128, 0, 0, 1),
    2,
    "settle",
    (-1, 1, 0, 128, 0, 0, 1),
    (-2, 1, 0, 128, 0, 0, 1),
    -3,
    1,
    (4, 1, 0, 128, 0, 0, 1),
    3,
    -1,
    -2,
    4,
)


def nearest(dz):
    dz %= Z
    return dz - Z if dz > Z // 2 else dz


class Gather:
    def __init__(self, place, buf, own, plan, send_sem, recv_sem):
        self.p, self.buf, self.own, self.plan = place, buf, own, plan
        self.send_sem, self.recv_sem = send_sem, recv_sem
        self.sends = [step for step in plan if isinstance(step, tuple)]
        self.brings = {}
        for i, (dz, dy, first, rows, tz, ty, tk) in enumerate(self.sends):
            for r in range(first, first + rows, 16):
                self.brings[nearest(dz - tz), dy ^ ty, tk, r] = i
        self.waited = set()
        self.sent = []
        self.settled = 0

    def copy(self, i, block, device):
        p = self.p
        dz, dy, dk = block
        first, rows = self.sends[i][2:4]
        here = self.buf.at[p.along(dz), (p.y + dy) % 2, (p.k + dk) % 2, pl.ds(first, rows)]
        mine = self.own is not None and block == (0, 0, 0)
        return pltpu.make_async_remote_copy(
            src_ref=self.own.at[pl.ds(first, rows)] if mine else here,
            dst_ref=here,
            send_sem=self.send_sem.at[i],
            recv_sem=self.recv_sem.at[i],
            device_id=device,
            device_id_type=MESH,
        )

    def need(self, block, first, rows):
        if block == (0, 0, 0):
            return
        for r in range(first, first + rows, 16):
            i = self.brings[block + (r,)]
            if i not in self.waited:
                self.waited.add(i)
                dz, dy, _, _, tz, ty, tk = self.sends[i]
                self.copy(i, (nearest(dz - tz), dy ^ ty, tk), self.p.to(0, 0, 1)).wait_recv()

    def run(self, on_chip, named):
        for step in self.plan:
            if isinstance(step, str):
                named[step]()
            elif isinstance(step, int):
                for block in ((step, 0, 0), (step, 1, 0), (step, 0, 1), (step, 1, 1)):
                    self.need(block, 0, ROWS)
                on_chip(self.p.along(step))
            else:
                dz, dy, first, rows, tz, ty, tk = step
                self.need((nearest(dz), dy, 0), first, rows)
                c = self.copy(len(self.sent), (dz, dy, 0), self.p.to(tz, ty, tk))
                c.start()
                self.sent.append(c)

    def settle(self, in_flight=0):
        upto = max(self.settled, len(self.sent) - in_flight)
        for c in self.sent[self.settled : upto]:
            c.wait_send()
        self.settled = upto


def kernel(
    tokens,
    gain_hbm,
    in_weight,
    filter_hbm,
    rows_hbm,
    decay_hbm,
    angle_hbm,
    residue_hbm,
    state_hbm,
    skip_hbm,
    out_weight,
    mixed,
    gain,
    short_filter,
    prior_rows,
    decay_rate,
    pole_angle,
    residue,
    skip_weight,
    own,
    wide,
    stats,
    weight,
    narrow,
    last_weight,
    power_re,
    power_im,
    lift_re,
    lift_im,
    response,
    total,
    rim,
    ext,
    padded,
    ends,
    incoming,
    shard_power,
    scales,
    hello,
    local_sem,
    send1,
    recv1,
    send2,
    recv2,
    small_send,
    small_recv,
):
    p = Place()
    barrier = pltpu.get_barrier_semaphore()
    kin = [
        (4 * (p.seq // 4) + (p.seq + 1) % 4, p.chan),
        (4 * (p.seq // 4) + (p.seq + 3) % 4, p.chan),
        ((p.seq + 4) % SEQ, p.chan),
    ]
    greeted = [p.to(*by) for by in ((0, 0, 1), (0, 1, 0), (0, 1, 1), (1, 0, 0), (-1, 0, 0), (2, 0, 0), (-2, 0, 0))]
    greeted += kin
    for device in greeted:
        pl.semaphore_signal(barrier, inc=1, device_id=device, device_id_type=MESH)

    pairs = (
        (tokens, own),
        (gain_hbm, gain),
        (filter_hbm, short_filter),
        (rows_hbm, prior_rows),
        (decay_hbm, decay_rate),
        (angle_hbm, pole_angle),
        (residue_hbm, residue),
        (state_hbm, incoming),
        (skip_hbm, skip_weight),
    )
    loads = [pltpu.make_async_copy(a, b, local_sem.at[4 + i]) for i, (a, b) in enumerate(pairs)]
    weight_loads = []
    for i in range(3):
        weight_loads.append(
            pltpu.make_async_copy(in_weight.at[i], weight.at[:, pl.ds(i * CH, CH)], local_sem.at[i])
        )
    last_load = pltpu.make_async_copy(out_weight, last_weight, local_sem.at[3])
    for c in loads + weight_loads + [last_load]:
        c.start()

    pl.semaphore_wait(barrier, len(greeted))

    def small(src, dst, index, device):
        return pltpu.make_async_remote_copy(
            src_ref=src,
            dst_ref=dst,
            send_sem=small_send.at[index],
            recv_sem=small_recv.at[index],
            device_id=device,
            device_id_type=MESH,
        )

    small_sent = []

    def spread_small(src, index, device):
        c = small(src, src, index, device)
        c.start()
        small_sent.append(c)

    def small_here(z, index):
        small(stats.at[z], stats.at[z], index, p.to(0, 0, 1)).wait_recv()

    pair = ((0, 1), (1, 0), (1, 1))

    def stats1():
        loads[0].wait()
        loads[1].wait()
        values = own[...].astype(F32)
        squares = jnp.sum(values * values, axis=1, keepdims=True)
        row = jnp.broadcast_to(squares, (ROWS, 128)).T
        gains = gain[...].astype(F32).reshape(1, FEATS)
        stats[p.z, 2 * p.y + p.k] = jnp.concatenate(
            [row[0:1], gains[:, 0:128], gains[:, 128:256], row[3:4]], axis=0
        )
        wide[p.z, p.y, p.k] = own[...]
        for i, (dy, dk) in enumerate(pair):
            spread_small(stats.at[p.z, 2 * p.y + p.k], i, p.to(0, dy, dk))
        for device in kin:
            pl.semaphore_signal(hello.at[0], inc=1, device_id=device, device_id_type=MESH)

    def stats2():
        for i, (dy, dk) in enumerate(pair):
            theirs = stats.at[p.z, 2 * ((p.y + dy) % 2) + (p.k + dk) % 2]
            small(theirs, theirs, i, p.to(0, dy, dk)).wait_recv()
        for i, by in enumerate((1, -1, 2, -2)):
            spread_small(stats.at[p.z], 3 + i, p.to(by, 0, 0))

    def stats3():
        for i, by in enumerate((3, -3, 4)):
            spread_small(stats.at[p.z], 7 + i, p.to(by, 0, 0))

    def tables():
        for c in loads[2:]:
            c.wait()
        magnitude = jnp.exp(-decay_rate[...])
        pole_re = magnitude * jnp.cos(pole_angle[...])
        pole_im = magnitude * jnp.sin(pole_angle[...])
        res_re = residue[0]
        res_im = residue[1]

        def tabulate(t, carry):
            re, im, lre, lim = carry
            power_re[t] = re
            power_im[t] = im
            response[pl.ds(8 + t, 1)] = jnp.sum(lre, axis=0, keepdims=True)
            lre, lim = pole_re * lre - pole_im * lim, pole_re * lim + pole_im * lre
            lift_re[t] = lre
            lift_im[t] = lim
            return (pole_re * re - pole_im * im, pole_re * im + pole_im * re, lre, lim)

        one = jnp.ones((MODES, CH), F32)
        end_re, end_im, _, _ = lax.fori_loop(
            0, ROWS, tabulate, (one, jnp.zeros_like(one), res_re, res_im)
        )
        padded[pl.ds(0, ROWS)] = jnp.zeros((ROWS, CH), F32)
        response[pl.ds(0, 8)] = jnp.zeros((8, CH), F32)
        total[...] = jnp.zeros_like(total)
        shard_power[0] = end_re
        shard_power[1] = end_im

    def find_scale():
        for i, by in enumerate((1, -1, 2, -2, 3, -3, 4)):
            small_here(p.along(-by), 3 + i)
        pl.semaphore_wait(hello.at[0], len(kin))
        for device in kin:
            pl.semaphore_signal(hello.at[1], inc=1, device_id=device, device_id_type=MESH)
        summed = jnp.zeros((1, 128), F32)
        for z in range(Z):
            for j in range(4):
                summed = summed + stats[z, j, 0:1]
        scale_row = lax.rsqrt(summed / (FEATS * 4 * Z) + EPSILON)
        scales[...] = jnp.broadcast_to(scale_row, (ROWS, 128)).T
        for c in weight_loads:
            c.wait()

    def project(z):
        parts = []
        scale = scales[...]
        for j in range(4):
            x = wide[z, j // 2, j % 2].astype(F32)
            for h in range(2):
                part = x[:, 128 * h : 128 * h + 128] * scale * stats[z, j, 1 + h : 2 + h]
                parts.append(part.astype(BF16))
        normed = jnp.concatenate(parts, axis=1)
        rows = weight[pl.ds(pl.multiple_of(z * 4 * FEATS, 4 * FEATS), 4 * FEATS)]
        total[...] += jnp.dot(normed, rows, preferred_element_type=F32)

    spread = Gather(p, wide, tokens, WIDE_PLAN, send1, recv1)
    spread.run(
        project,
        {"stats1": stats1, "tables": tables, "stats2": stats2, "stats3": stats3, "scale": find_scale},
    )

    def close_spread():
        for c in small_sent:
            c.wait_send()
        spread.settle()

    projected = total[...].astype(BF16).astype(F32)
    ext[pl.ds(0, 8)] = jnp.zeros((8, 3 * CH), F32)
    ext[pl.ds(8, ROWS)] = projected

    def convolve(i):
        lanes = pl.ds(i * CH, CH)
        c = jnp.zeros((ROWS, CH), F32)
        for lag in range(3):
            c = c + short_filter[lag, i : i + 1] * ext[pl.ds(8 - lag, ROWS), lanes]
        return c

    key, value = convolve(1), convolve(2)
    row_of = lax.broadcasted_iota(jnp.int32, (ROWS, CH), 0)
    drive = jnp.where(row_of < 2, 0.0, key * value)
    padded[pl.ds(ROWS, ROWS)] = drive

    nothing = jnp.zeros((MODES, CH), F32)
    sums = [[nothing, nothing] for _ in range(4)]
    for t in range(2, ROWS):
        u = padded[pl.ds(ROWS + t, 1)]
        sums[t % 4][0] += power_re[ROWS - 1 - t] * u
        sums[t % 4][1] += power_im[ROWS - 1 - t] * u

    edges = [projected[ROWS - 2 :, i * CH : i * CH + CH] for i in range(3)]
    edges += [jnp.zeros((2, CH), F32), key[0:2], value[0:2], jnp.zeros((4, CH), F32)]
    ends[p.seq, pl.ds(0, MODES)] = sums[0][0] + sums[1][0] + sums[2][0] + sums[3][0]
    ends[p.seq, pl.ds(MODES, MODES)] = sums[0][1] + sums[1][1] + sums[2][1] + sums[3][1]
    ends[p.seq, pl.ds(2 * MODES, 16)] = jnp.concatenate(edges, axis=0)
    here = ends.at[p.seq]

    def end_copy(i):
        return small(here, here, 10 + i, ((p.seq + i) % SEQ, p.chan))

    pl.semaphore_wait(hello.at[1], len(kin))
    for i in (6, 5, 7, 4, 2, 3, 1):

        @pl.when(p.seq + i < SEQ)
        def _():
            end_copy(i).start()

    def close_state():
        for i in range(1, SEQ):

            @pl.when(p.seq + i < SEQ)
            def _():
                end_copy(i).wait_send()

    query = convolve(0)

    def respond(i, acc):
        for j in range(4):
            lag = 4 * i + j
            acc = acc + response[pl.ds(8 + lag, 1)] * padded[pl.ds(ROWS - lag, ROWS)]
        return acc

    mode_out = lax.fori_loop(0, ROWS // 4, respond, jnp.zeros((ROWS, CH), F32))
    close_spread()

    def first_rows(i, so_far):
        near, far = short_filter[1, i : i + 1], short_filter[2, i : i + 1]
        before = rim[pl.ds(2 * i, 2)]
        return (
            so_far[0:1] + near * before[1:2] + far * before[0:1],
            so_far[1:2] + far * before[1:2],
        )

    def first_drive(key_rows, value_rows):
        (key0, key1), (value0, value1) = first_rows(1, key_rows), first_rows(2, value_rows)
        return key0 * value0, key1 * value1

    for i in range(3):
        rim[pl.ds(2 * i, 2)] = prior_rows[i].astype(F32)
    shard_re, shard_im = shard_power[0], shard_power[1]
    last_re, last_im = power_re[ROWS - 1], power_im[ROWS - 1]
    next_re, next_im = power_re[ROWS - 2], power_im[ROWS - 2]
    for j in range(SEQ - 1):

        @pl.when(j < p.seq)
        def _():
            theirs = ends.at[j]
            for i in range(1, SEQ):

                @pl.when(p.seq - j == i)
                def _():
                    small(theirs, theirs, 10 + i, (j, p.chan)).wait_recv()

            drive0, drive1 = first_drive(ends[j, pl.ds(40, 2)], ends[j, pl.ds(42, 2)])
            re, im = incoming[0], incoming[1]
            end_re = ends[j, pl.ds(0, MODES)] + last_re * drive0 + next_re * drive1
            end_im = ends[j, pl.ds(MODES, MODES)] + last_im * drive0 + next_im * drive1
            incoming[0] = shard_re * re - shard_im * im + end_re
            incoming[1] = shard_re * im + shard_im * re + end_im
            rim[pl.ds(0, 6)] = ends[j, pl.ds(32, 6)]

    in_re, in_im = incoming[0], incoming[1]
    carried = []
    for b in range(ROWS // 8):
        lre = lift_re[pl.ds(8 * b, 8)]
        lim = lift_im[pl.ds(8 * b, 8)]
        carried.append(jnp.sum(lre * in_re[None] - lim * in_im[None], axis=1))
    drive0, drive1 = first_drive(key[0:2], value[0:2])
    query0, query1 = first_rows(0, query[0:2])
    first, second = row_of == 0, row_of == 1
    drive = jnp.where(first, drive0, jnp.where(second, drive1, drive))
    query = jnp.where(first, query0, jnp.where(second, query1, query))
    mode_out = mode_out + response[pl.ds(8, ROWS)] * drive0 + response[pl.ds(7, ROWS)] * drive1
    mode_out = mode_out + jnp.concatenate(carried, axis=0)
    narrow[p.z, p.y, p.k] = (query * (mode_out + skip_weight[...] * drive)).astype(BF16)

    def begin():
        total[:, pl.ds(0, FEATS)] = own[...].astype(F32)
        last_load.wait()

    def output(z):
        parts = [narrow[z, j // 2, j % 2] for j in range(4)]
        rows = last_weight[pl.ds(pl.multiple_of(z * 4 * CH, 4 * CH), 4 * CH)]
        total[:, pl.ds(0, FEATS)] += jnp.dot(
            jnp.concatenate(parts, axis=1), rows, preferred_element_type=F32
        )

    mix = Gather(p, narrow, None, NARROW_PLAN, send2, recv2)

    def settle():
        if not mix.settled:
            close_state()
        mix.settle(in_flight=8)

    mix.run(output, {"begin": begin, "settle": settle})
    mixed[...] = total[:, pl.ds(0, FEATS)].astype(BF16)

    mix.settle()


def body(
    tokens,
    norm_gain,
    in_weight,
    short_filter,
    prior_rows,
    decay_rate,
    pole_angle,
    residue,
    prior_state,
    skip_weight,
    out_weight,
):
    vmem = pl.BlockSpec(memory_space=pltpu.VMEM)
    hbm = pl.BlockSpec(memory_space=pltpu.HBM)
    flops = 2 * ROWS * (FEATS * 32 * 3 * CH + CH * 32 * FEATS)
    return pl.pallas_call(
        kernel,
        out_shape=jax.ShapeDtypeStruct((ROWS, FEATS), BF16),
        in_specs=[hbm] * 11,
        out_specs=vmem,
        scratch_shapes=[
            pltpu.VMEM((FEATS,), BF16),
            pltpu.VMEM((3, 3, CH), F32),
            pltpu.VMEM((3, 2, CH), BF16),
            pltpu.VMEM((MODES, CH), F32),
            pltpu.VMEM((MODES, CH), F32),
            pltpu.VMEM((2, MODES, CH), F32),
            pltpu.VMEM((1, CH), F32),
            pltpu.VMEM((ROWS, FEATS), BF16),
            pltpu.VMEM((Z, 2, 2, ROWS, FEATS), BF16),
            pltpu.VMEM((Z, 4, 4, 128), F32),
            pltpu.VMEM((Z * 4 * FEATS, 3 * CH), BF16),
            pltpu.VMEM((Z, 2, 2, ROWS, CH), BF16),
            pltpu.VMEM((Z * 4 * CH, FEATS), BF16),
            pltpu.VMEM((ROWS, MODES, CH), F32),
            pltpu.VMEM((ROWS, MODES, CH), F32),
            pltpu.VMEM((ROWS, MODES, CH), F32),
            pltpu.VMEM((ROWS, MODES, CH), F32),
            pltpu.VMEM((8 + ROWS, CH), F32),
            pltpu.VMEM((ROWS, 3 * CH), F32),
            pltpu.VMEM((8, CH), F32),
            pltpu.VMEM((8 + ROWS, 3 * CH), F32),
            pltpu.VMEM((2 * ROWS, CH), F32),
            pltpu.VMEM((SEQ, 2 * MODES + 16, CH), F32),
            pltpu.VMEM((2, MODES, CH), F32),
            pltpu.VMEM((2, MODES, CH), F32),
            pltpu.VMEM((ROWS, 128), F32),
            pltpu.SemaphoreType.REGULAR((2,)),
            pltpu.SemaphoreType.DMA((13,)),
            pltpu.SemaphoreType.DMA((len(WIDE_PLAN),)),
            pltpu.SemaphoreType.DMA((len(WIDE_PLAN),)),
            pltpu.SemaphoreType.DMA((len(NARROW_PLAN),)),
            pltpu.SemaphoreType.DMA((len(NARROW_PLAN),)),
            pltpu.SemaphoreType.DMA((18,)),
            pltpu.SemaphoreType.DMA((18,)),
        ],
        compiler_params=pltpu.CompilerParams(
            collective_id=0, has_side_effects=True, vmem_limit_bytes=60 * 1024 * 1024
        ),
        cost_estimate=pl.CostEstimate(flops=flops, bytes_accessed=9 * 1024 * 1024, transcendentals=0),
    )(
        tokens,
        norm_gain,
        jnp.transpose(in_weight, (1, 0, 2)),
        short_filter,
        jnp.transpose(prior_rows, (1, 0, 2)),
        decay_rate.T,
        pole_angle.T,
        jnp.transpose(residue, (0, 2, 1)),
        jnp.transpose(prior_state, (0, 2, 1)),
        skip_weight.reshape(1, CH),
        out_weight,
    )


def solution(mesh):
    return jax.shard_map(
        body,
        mesh=mesh,
        in_specs=(
            P("seq", "chan"),
            P("chan"),
            P(None, None, "chan"),
            P(None, None, "chan"),
            P(None, None, "chan"),
            P("chan", None),
            P("chan", None),
            P(None, "chan", None),
            P(None, "chan", None),
            P("chan"),
            P(None, "chan"),
        ),
        out_specs=P("seq", "chan"),
        check_vma=False,
    )
```

```python
import jax
import jax.numpy as jnp
from jax import lax
from jax.experimental import pallas as pl
from jax.experimental.pallas import tpu as pltpu
from jax.sharding import PartitionSpec as P

MESH = pl.DeviceIdType.MESH
EPSILON = 1e-06
F32 = jnp.float32
BF16 = jnp.bfloat16

Z = 8
ROWS = 128
FEATS = 256
CH = 128
MODES = 16
SEQ = 8


class Place:
    def __init__(self):
        self.seq = lax.axis_index("seq")
        chan = lax.axis_index("chan")
        self.chan = chan
        self.z = chan // 4
        self.y = (chan // 2) % 2
        self.k = chan % 2

    def at(self, z, y, k):
        return (self.seq, z * 4 + y * 2 + k)

    def to(self, dz, dy, dk):
        return self.at(self.along(dz), (self.y + dy) % 2, (self.k + dk) % 2)

    def along(self, by):
        return (self.z + by + Z) % Z


WIDE_PLAN = (
    (0, 0, 0, 128, 2, 0, 0),
    (0, 0, 0, 128, -2, 0, 0),
    (0, 0, 0, 128, 1, 0, 0),
    (0, 0, 0, 128, -1, 0, 0),
    (0, 0, 0, 128, 0, 1, 0),
    (0, 0, 0, 128, 0, 0, 1),
    "stats1",
    "tables",
    (0, 1, 64, 64, 2, 0, 0),
    (0, 1, 64, 64, -2, 0, 0),
    (0, 1, 0, 128, 0, 0, 1),
    (-2, 0, 32, 32, 2, 0, 0),
    (2, 0, 0, 32, -2, 0, 0),
    (-2, 0, 96, 32, 2, 0, 0),
    (-2, 0, 0, 96, 1, 0, 0),
    (2, 0, 0, 96, -1, 0, 0),
    (-2, 0, 0, 64, 0, 1, 0),
    (2, 0, 0, 64, 0, 1, 0),
    (-2, 0, 0, 128, 0, 0, 1),
    (2, 0, 0, 128, 0, 0, 1),
    (-1, 0, 96, 32, 2, 0, 0),
    (1, 0, 64, 32, -3, 0, 0),
    (1, 0, 96, 32, -2, 0, 0),
    (-1, 0, 0, 128, 0, 1, 0),
    "stats2",
    "stats3",
    (1, 0, 0, 128, 0, 1, 0),
    (-1, 0, 0, 128, 0, 0, 1),
    (1, 0, 0, 128, 0, 0, 1),
    (-2, 1, 96, 32, 2, 0, 0),
    (2, 1, 64, 32, -2, 0, 0),
    (-2, 1, 0, 128, 1, 0, 0),
    (-2, 1, 0, 128, 0, 0, 1),
    (4, 0, 0, 64, 0, 1, 0),
    (2, 1, 32, 96, -1, 0, 0),
    (2, 1, 0, 128, 0, 0, 1),
    (3, 0, 0, 32, 0, 1, 0),
    (-1, 1, 0, 128, 0, 0, 1),
    (-3, 0, 0, 128, 0, 0, 1),
    (4, 0, 0, 128, 0, 0, 1),
    (3, 0, 0, 128, 0, 0, 1),
    (1, 1, 0, 128, 0, 0, 1),
    (4, 1, 0, 128, 0, 0, 1),
    (-3, 1, 0, 128, 0, 0, 1),
    (3, 1, 0, 128, 0, 0, 1),
    "scale",
    0,
    -2,
    2,
    -1,
    1,
    4,
    -3,
    3,
)

NARROW_PLAN = (
    (0, 0, 0, 64, 4, 1, 0),
    (0, 0, 0, 128, -3, 0, 0),
    (0, 0, 0, 128, 3, 0, 0),
    (0, 0, 0, 128, -1, 0, 0),
    (0, 0, 0, 128, 1, 0, 0),
    (0, 0, 0, 128, 0, 1, 0),
    (0, 0, 0, 128, 0, 0, 1),
    "begin",
    (0, 1, 64, 64, 4, 0, 0),
    (0, 1, 0, 128, -2, 0, 0),
    (0, 1, 0, 128, 2, 0, 0),
    (0, 1, 0, 128, -1, 0, 0),
    (0, 1, 0, 128, 1, 0, 0),
    (0, 1, 0, 128, 0, 0, 1),
    0,
    (3, 0, 0, 128, -1, 0, 0),
    (3, 0, 0, 128, 0, 1, 0),
    (3, 0, 0, 128, 0, 0, 1),
    (1, 0, 0, 128, -1, 0, 0),
    (1, 0, 0, 128, -1, 0, 1),
    (1, 0, 0, 128, 0, 0, 1),
    (-3, 0, 0, 128, 0, 1, 0),
    (-3, 0, 0, 128, 0, 1, 1),
    (-3, 0, 0, 128, 0, 0, 1),
    (-1, 0, 0, 128, 1, 0, 0),
    (-1, 0, 0, 128, 1, 0, 1),
    "settle",
    (-1, 0, 0, 128, 0, 0, 1),
    (2, 1, 0, 128, 0, 0, 1),
    (1, 1, 0, 128, 0, 0, 1),
    (3, 1, 0, 128, 0, 0, 1),
    "settle",
    (4, 0, 0, 128, 0, 0, 1),
    (4, 1, 0, 128, 0, 0, 1),
    (-2, 1, 0, 128, 0, 0, 1),
    1,
    (-1, 1, 0, 128, 0, 0, 1),
    3,
    2,
    4,
    -3,
    -1,
    -2,
)


def nearest(dz):
    dz %= Z
    return dz - Z if dz > Z // 2 else dz


class Gather:
    def __init__(self, place, buf, own, plan, send_sem, recv_sem):
        self.p, self.buf, self.own, self.plan = place, buf, own, plan
        self.send_sem, self.recv_sem = send_sem, recv_sem
        self.sends = [step for step in plan if isinstance(step, tuple)]
        self.brings = {}
        for i, (dz, dy, first, rows, tz, ty, tk) in enumerate(self.sends):
            for r in range(first, first + rows, 16):
                self.brings[nearest(dz - tz), dy ^ ty, tk, r] = i
        self.waited = set()
        self.sent = []
        self.settled = 0

    def copy(self, i, block, device):
        p = self.p
        dz, dy, dk = block
        first, rows = self.sends[i][2:4]
        here = self.buf.at[p.along(dz), (p.y + dy) % 2, (p.k + dk) % 2, pl.ds(first, rows)]
        mine = self.own is not None and block == (0, 0, 0)
        return pltpu.make_async_remote_copy(
            src_ref=self.own.at[pl.ds(first, rows)] if mine else here,
            dst_ref=here,
            send_sem=self.send_sem.at[i],
            recv_sem=self.recv_sem.at[i],
            device_id=device,
            device_id_type=MESH,
        )

    def need(self, block, first, rows):
        if block == (0, 0, 0):
            return
        for r in range(first, first + rows, 16):
            i = self.brings[block + (r,)]
            if i not in self.waited:
                self.waited.add(i)
                dz, dy, _, _, tz, ty, tk = self.sends[i]
                self.copy(i, (nearest(dz - tz), dy ^ ty, tk), self.p.to(0, 0, 1)).wait_recv()

    def run(self, on_chip, named):
        for step in self.plan:
            if isinstance(step, str):
                named[step]()
            elif isinstance(step, int):
                for block in ((step, 0, 0), (step, 1, 0), (step, 0, 1), (step, 1, 1)):
                    self.need(block, 0, ROWS)
                on_chip(self.p.along(step))
            else:
                dz, dy, first, rows, tz, ty, tk = step
                self.need((nearest(dz), dy, 0), first, rows)
                c = self.copy(len(self.sent), (dz, dy, 0), self.p.to(tz, ty, tk))
                c.start()
                self.sent.append(c)

    def settle(self, in_flight=0):
        upto = max(self.settled, len(self.sent) - in_flight)
        for c in self.sent[self.settled : upto]:
            c.wait_send()
        self.settled = upto


def kernel(
    tokens,
    gain_hbm,
    in_weight,
    filter_hbm,
    rows_hbm,
    decay_hbm,
    angle_hbm,
    residue_hbm,
    state_hbm,
    skip_hbm,
    out_weight,
    mixed,
    gain,
    short_filter,
    prior_rows,
    decay_rate,
    pole_angle,
    residue,
    skip_weight,
    own,
    wide,
    stats,
    weight,
    narrow,
    last_weight,
    power_re,
    power_im,
    lift_re,
    lift_im,
    response,
    total,
    rim,
    ext,
    padded,
    ends,
    query_out,
    query_in,
    incoming,
    shard_power,
    scales,
    hello,
    local_sem,
    send1,
    recv1,
    send2,
    recv2,
    small_send,
    small_recv,
):
    p = Place()
    barrier = pltpu.get_barrier_semaphore()
    kin = [
        (4 * (p.seq // 4) + (p.seq + 1) % 4, p.chan),
        (4 * (p.seq // 4) + (p.seq + 3) % 4, p.chan),
        ((p.seq + 4) % SEQ, p.chan),
    ]
    greeted = [p.to(*by) for by in ((0, 0, 1), (0, 1, 0), (0, 1, 1), (1, 0, 0), (-1, 0, 0), (2, 0, 0), (-2, 0, 0))]
    greeted += kin
    for device in greeted:
        pl.semaphore_signal(barrier, inc=1, device_id=device, device_id_type=MESH)

    pairs = (
        (tokens, own),
        (gain_hbm, gain),
        (filter_hbm, short_filter),
        (rows_hbm, prior_rows),
        (decay_hbm, decay_rate),
        (angle_hbm, pole_angle),
        (residue_hbm, residue),
        (state_hbm, incoming),
        (skip_hbm, skip_weight),
    )
    loads = [pltpu.make_async_copy(a, b, local_sem.at[4 + i]) for i, (a, b) in enumerate(pairs)]
    weight_loads = []
    for i in range(3):
        weight_loads.append(
            pltpu.make_async_copy(in_weight.at[i], weight.at[:, pl.ds(i * CH, CH)], local_sem.at[i])
        )
    last_load = pltpu.make_async_copy(out_weight, last_weight, local_sem.at[3])
    for c in loads + weight_loads + [last_load]:
        c.start()

    pl.semaphore_wait(barrier, len(greeted))

    def small(src, dst, index, device):
        return pltpu.make_async_remote_copy(
            src_ref=src,
            dst_ref=dst,
            send_sem=small_send.at[index],
            recv_sem=small_recv.at[index],
            device_id=device,
            device_id_type=MESH,
        )

    small_sent = []

    def spread_small(src, index, device):
        c = small(src, src, index, device)
        c.start()
        small_sent.append(c)

    def small_here(z, index):
        small(stats.at[z], stats.at[z], index, p.to(0, 0, 1)).wait_recv()

    pair = ((0, 1), (1, 0), (1, 1))

    def stats1():
        loads[0].wait()
        loads[1].wait()
        values = own[...].astype(F32)
        squares = jnp.sum(values * values, axis=1, keepdims=True)
        row = jnp.broadcast_to(squares, (ROWS, 128)).T
        gains = gain[...].astype(F32).reshape(1, FEATS)
        stats[p.z, 2 * p.y + p.k] = jnp.concatenate(
            [row[0:1], gains[:, 0:128], gains[:, 128:256], row[3:4]], axis=0
        )
        wide[p.z, p.y, p.k] = own[...]
        for i, (dy, dk) in enumerate(pair):
            spread_small(stats.at[p.z, 2 * p.y + p.k], i, p.to(0, dy, dk))
        for device in kin:
            pl.semaphore_signal(hello.at[0], inc=1, device_id=device, device_id_type=MESH)

    def stats2():
        for i, (dy, dk) in enumerate(pair):
            theirs = stats.at[p.z, 2 * ((p.y + dy) % 2) + (p.k + dk) % 2]
            small(theirs, theirs, i, p.to(0, dy, dk)).wait_recv()
        for i, by in enumerate((1, -1, 2, -2)):
            spread_small(stats.at[p.z], 3 + i, p.to(by, 0, 0))

    def stats3():
        for i, by in enumerate((3, -3, 4)):
            spread_small(stats.at[p.z], 7 + i, p.to(by, 0, 0))

    def tables():
        for c in loads[2:]:
            c.wait()
        magnitude = jnp.exp(-decay_rate[...])
        pole_re = magnitude * jnp.cos(pole_angle[...])
        pole_im = magnitude * jnp.sin(pole_angle[...])
        res_re = residue[0]
        res_im = residue[1]

        def tabulate(t, carry):
            re, im, lre, lim = carry
            power_re[t] = re
            power_im[t] = im
            response[pl.ds(8 + t, 1)] = jnp.sum(lre, axis=0, keepdims=True)
            lre, lim = pole_re * lre - pole_im * lim, pole_re * lim + pole_im * lre
            lift_re[t] = lre
            lift_im[t] = lim
            return (pole_re * re - pole_im * im, pole_re * im + pole_im * re, lre, lim)

        one = jnp.ones((MODES, CH), F32)
        end_re, end_im, _, _ = lax.fori_loop(
            0, ROWS, tabulate, (one, jnp.zeros_like(one), res_re, res_im)
        )
        padded[pl.ds(0, ROWS)] = jnp.zeros((ROWS, CH), F32)
        response[pl.ds(0, 8)] = jnp.zeros((8, CH), F32)
        total[...] = jnp.zeros_like(total)
        shard_power[0] = end_re
        shard_power[1] = end_im

    def find_scale():
        for i, by in enumerate((1, -1, 2, -2, 3, -3, 4)):
            small_here(p.along(-by), 3 + i)
        pl.semaphore_wait(hello.at[0], len(kin))
        for device in kin:
            pl.semaphore_signal(hello.at[1], inc=1, device_id=device, device_id_type=MESH)
        summed = jnp.zeros((1, 128), F32)
        for z in range(Z):
            for j in range(4):
                summed = summed + stats[z, j, 0:1]
        scale_row = lax.rsqrt(summed / (FEATS * 4 * Z) + EPSILON)
        scales[...] = jnp.broadcast_to(scale_row, (ROWS, 128)).T
        for c in weight_loads:
            c.wait()

    def project(z):
        parts = []
        scale = scales[...]
        for j in range(4):
            x = wide[z, j // 2, j % 2].astype(F32)
            for h in range(2):
                part = x[:, 128 * h : 128 * h + 128] * scale * stats[z, j, 1 + h : 2 + h]
                parts.append(part.astype(BF16))
        normed = jnp.concatenate(parts, axis=1)
        rows = weight[pl.ds(pl.multiple_of(z * 4 * FEATS, 4 * FEATS), 4 * FEATS)]
        total[...] += jnp.dot(normed, rows, preferred_element_type=F32)

    spread = Gather(p, wide, tokens, WIDE_PLAN, send1, recv1)
    spread.run(
        project,
        {"stats1": stats1, "tables": tables, "stats2": stats2, "stats3": stats3, "scale": find_scale},
    )

    def close_spread():
        for c in small_sent:
            c.wait_send()
        spread.settle()

    projected = total[...].astype(BF16).astype(F32)
    ext[pl.ds(0, 8)] = jnp.zeros((8, 3 * CH), F32)
    ext[pl.ds(8, ROWS)] = projected

    def convolve(i):
        lanes = pl.ds(i * CH, CH)
        c = jnp.zeros((ROWS, CH), F32)
        for lag in range(3):
            c = c + short_filter[lag, i : i + 1] * ext[pl.ds(8 - lag, ROWS), lanes]
        return c

    key, value = convolve(1), convolve(2)
    row_of = lax.broadcasted_iota(jnp.int32, (ROWS, CH), 0)
    drive = jnp.where(row_of < 2, 0.0, key * value)
    padded[pl.ds(ROWS, ROWS)] = drive

    nothing = jnp.zeros((MODES, CH), F32)
    sums = [[nothing, nothing] for _ in range(4)]
    for t in range(2, ROWS):
        u = padded[pl.ds(ROWS + t, 1)]
        sums[t % 4][0] += power_re[ROWS - 1 - t] * u
        sums[t % 4][1] += power_im[ROWS - 1 - t] * u

    edges = [projected[ROWS - 2 :, i * CH : i * CH + CH] for i in (1, 2)] + [key[0:2], value[0:2]]
    ends[p.seq, pl.ds(0, MODES)] = sums[0][0] + sums[1][0] + sums[2][0] + sums[3][0]
    ends[p.seq, pl.ds(MODES, MODES)] = sums[0][1] + sums[1][1] + sums[2][1] + sums[3][1]
    ends[p.seq, pl.ds(2 * MODES, 8)] = jnp.concatenate(edges, axis=0)
    here = ends.at[p.seq]

    def end_copy(i):
        return small(here, here, 10 + i, ((p.seq + i) % SEQ, p.chan))

    pl.semaphore_wait(hello.at[1], len(kin))
    for i in (6, 5, 7, 4, 2, 3, 1):

        @pl.when(p.seq + i < SEQ)
        def _():
            end_copy(i).start()

    query_out[...] = projected[ROWS - 8 :, 0:CH]
    query_copy = small(query_out, query_in, 10, ((p.seq + 1) % SEQ, p.chan))

    @pl.when(p.seq < SEQ - 1)
    def _():
        query_copy.start()

    def close_state():
        @pl.when(p.seq < SEQ - 1)
        def _():
            query_copy.wait_send()

        for i in range(1, SEQ):

            @pl.when(p.seq + i < SEQ)
            def _():
                end_copy(i).wait_send()

    query = convolve(0)

    def respond(i, acc):
        for j in range(4):
            lag = 4 * i + j
            acc = acc + response[pl.ds(8 + lag, 1)] * padded[pl.ds(ROWS - lag, ROWS)]
        return acc

    mode_out = lax.fori_loop(0, ROWS // 4, respond, jnp.zeros((ROWS, CH), F32))
    close_spread()

    def first_rows(i, so_far):
        near, far = short_filter[1, i : i + 1], short_filter[2, i : i + 1]
        before = rim[pl.ds(2 * i, 2)]
        return (
            so_far[0:1] + near * before[1:2] + far * before[0:1],
            so_far[1:2] + far * before[1:2],
        )

    def first_drive(key_rows, value_rows):
        (key0, key1), (value0, value1) = first_rows(1, key_rows), first_rows(2, value_rows)
        return key0 * value0, key1 * value1

    for i in range(3):
        rim[pl.ds(2 * i, 2)] = prior_rows[i].astype(F32)

    @pl.when(p.seq > 0)
    def _():
        query_copy.wait_recv()
        rim[pl.ds(0, 2)] = query_in[pl.ds(6, 2)]

    shard_re, shard_im = shard_power[0], shard_power[1]
    last_re, last_im = power_re[ROWS - 1], power_im[ROWS - 1]
    next_re, next_im = power_re[ROWS - 2], power_im[ROWS - 2]
    for j in range(SEQ - 1):

        @pl.when(j < p.seq)
        def _():
            theirs = ends.at[j]
            for i in range(1, SEQ):

                @pl.when(p.seq - j == i)
                def _():
                    small(theirs, theirs, 10 + i, (j, p.chan)).wait_recv()

            drive0, drive1 = first_drive(ends[j, pl.ds(36, 2)], ends[j, pl.ds(38, 2)])
            re, im = incoming[0], incoming[1]
            end_re = ends[j, pl.ds(0, MODES)] + last_re * drive0 + next_re * drive1
            end_im = ends[j, pl.ds(MODES, MODES)] + last_im * drive0 + next_im * drive1
            incoming[0] = shard_re * re - shard_im * im + end_re
            incoming[1] = shard_re * im + shard_im * re + end_im
            rim[pl.ds(2, 4)] = ends[j, pl.ds(32, 4)]

    in_re, in_im = incoming[0], incoming[1]
    carried = []
    for b in range(ROWS // 8):
        lre = lift_re[pl.ds(8 * b, 8)]
        lim = lift_im[pl.ds(8 * b, 8)]
        carried.append(jnp.sum(lre * in_re[None] - lim * in_im[None], axis=1))
    drive0, drive1 = first_drive(key[0:2], value[0:2])
    query0, query1 = first_rows(0, query[0:2])
    first, second = row_of == 0, row_of == 1
    drive = jnp.where(first, drive0, jnp.where(second, drive1, drive))
    query = jnp.where(first, query0, jnp.where(second, query1, query))
    mode_out = mode_out + response[pl.ds(8, ROWS)] * drive0 + response[pl.ds(7, ROWS)] * drive1
    mode_out = mode_out + jnp.concatenate(carried, axis=0)
    narrow[p.z, p.y, p.k] = (query * (mode_out + skip_weight[...] * drive)).astype(BF16)

    def begin():
        total[:, pl.ds(0, FEATS)] = own[...].astype(F32)
        last_load.wait()

    def output(z):
        parts = [narrow[z, j // 2, j % 2] for j in range(4)]
        rows = last_weight[pl.ds(pl.multiple_of(z * 4 * CH, 4 * CH), 4 * CH)]
        total[:, pl.ds(0, FEATS)] += jnp.dot(
            jnp.concatenate(parts, axis=1), rows, preferred_element_type=F32
        )

    mix = Gather(p, narrow, None, NARROW_PLAN, send2, recv2)

    def settle():
        if not mix.settled:
            close_state()
        mix.settle(in_flight=8)

    mix.run(output, {"begin": begin, "settle": settle})
    mixed[...] = total[:, pl.ds(0, FEATS)].astype(BF16)

    mix.settle()


def body(
    tokens,
    norm_gain,
    in_weight,
    short_filter,
    prior_rows,
    decay_rate,
    pole_angle,
    residue,
    prior_state,
    skip_weight,
    out_weight,
):
    vmem = pl.BlockSpec(memory_space=pltpu.VMEM)
    hbm = pl.BlockSpec(memory_space=pltpu.HBM)
    flops = 2 * ROWS * (FEATS * 32 * 3 * CH + CH * 32 * FEATS)
    return pl.pallas_call(
        kernel,
        out_shape=jax.ShapeDtypeStruct((ROWS, FEATS), BF16),
        in_specs=[hbm] * 11,
        out_specs=vmem,
        scratch_shapes=[
            pltpu.VMEM((FEATS,), BF16),
            pltpu.VMEM((3, 3, CH), F32),
            pltpu.VMEM((3, 2, CH), BF16),
            pltpu.VMEM((MODES, CH), F32),
            pltpu.VMEM((MODES, CH), F32),
            pltpu.VMEM((2, MODES, CH), F32),
            pltpu.VMEM((1, CH), F32),
            pltpu.VMEM((ROWS, FEATS), BF16),
            pltpu.VMEM((Z, 2, 2, ROWS, FEATS), BF16),
            pltpu.VMEM((Z, 4, 4, 128), F32),
            pltpu.VMEM((Z * 4 * FEATS, 3 * CH), BF16),
            pltpu.VMEM((Z, 2, 2, ROWS, CH), BF16),
            pltpu.VMEM((Z * 4 * CH, FEATS), BF16),
            pltpu.VMEM((ROWS, MODES, CH), F32),
            pltpu.VMEM((ROWS, MODES, CH), F32),
            pltpu.VMEM((ROWS, MODES, CH), F32),
            pltpu.VMEM((ROWS, MODES, CH), F32),
            pltpu.VMEM((8 + ROWS, CH), F32),
            pltpu.VMEM((ROWS, 3 * CH), F32),
            pltpu.VMEM((8, CH), F32),
            pltpu.VMEM((8 + ROWS, 3 * CH), F32),
            pltpu.VMEM((2 * ROWS, CH), F32),
            pltpu.VMEM((SEQ, 2 * MODES + 8, CH), F32),
            pltpu.VMEM((8, CH), F32),
            pltpu.VMEM((8, CH), F32),
            pltpu.VMEM((2, MODES, CH), F32),
            pltpu.VMEM((2, MODES, CH), F32),
            pltpu.VMEM((ROWS, 128), F32),
            pltpu.SemaphoreType.REGULAR((2,)),
            pltpu.SemaphoreType.DMA((13,)),
            pltpu.SemaphoreType.DMA((len(WIDE_PLAN),)),
            pltpu.SemaphoreType.DMA((len(WIDE_PLAN),)),
            pltpu.SemaphoreType.DMA((len(NARROW_PLAN),)),
            pltpu.SemaphoreType.DMA((len(NARROW_PLAN),)),
            pltpu.SemaphoreType.DMA((18,)),
            pltpu.SemaphoreType.DMA((18,)),
        ],
        compiler_params=pltpu.CompilerParams(
            collective_id=0, has_side_effects=True, vmem_limit_bytes=60 * 1024 * 1024
        ),
        cost_estimate=pl.CostEstimate(flops=flops, bytes_accessed=9 * 1024 * 1024, transcendentals=0),
    )(
        tokens,
        norm_gain,
        jnp.transpose(in_weight, (1, 0, 2)),
        short_filter,
        jnp.transpose(prior_rows, (1, 0, 2)),
        decay_rate.T,
        pole_angle.T,
        jnp.transpose(residue, (0, 2, 1)),
        jnp.transpose(prior_state, (0, 2, 1)),
        skip_weight.reshape(1, CH),
        out_weight,
    )


def solution(mesh):
    return jax.shard_map(
        body,
        mesh=mesh,
        in_specs=(
            P("seq", "chan"),
            P("chan"),
            P(None, None, "chan"),
            P(None, None, "chan"),
            P(None, None, "chan"),
            P("chan", None),
            P("chan", None),
            P(None, "chan", None),
            P(None, "chan", None),
            P("chan"),
            P(None, "chan"),
        ),
        out_specs=P("seq", "chan"),
        check_vma=False,
    )
```

```python
import jax
import jax.numpy as jnp
from jax import lax
from jax.experimental import pallas as pl
from jax.experimental.pallas import tpu as pltpu
from jax.sharding import PartitionSpec as P

MESH = pl.DeviceIdType.MESH
EPSILON = 1e-06
F32 = jnp.float32
BF16 = jnp.bfloat16

Z = 8
ROWS = 128
FEATS = 256
CH = 128
MODES = 16
SEQ = 8


class Place:
    def __init__(self):
        self.seq = lax.axis_index("seq")
        chan = lax.axis_index("chan")
        self.chan = chan
        self.z = chan // 4
        self.y = (chan // 2) % 2
        self.k = chan % 2

    def at(self, z, y, k):
        return (self.seq, z * 4 + y * 2 + k)

    def to(self, dz, dy, dk):
        return self.at(self.along(dz), (self.y + dy) % 2, (self.k + dk) % 2)

    def along(self, by):
        return (self.z + by + Z) % Z


WIDE_PLAN = (
    (0, 0, 0, 128, -2, 0, 0),
    (0, 0, 0, 128, 2, 0, 0),
    (0, 0, 0, 128, -1, 0, 0),
    (0, 0, 0, 128, 1, 0, 0),
    (0, 0, 0, 128, 0, 1, 0),
    (0, 0, 0, 128, 0, 1, 1),
    (0, 0, 0, 128, 0, 0, 1),
    "stats1",
    (0, 1, 64, 64, -2, 0, 0),
    (0, 1, 64, 64, 2, 0, 0),
    "tables",
    (2, 0, 32, 32, -2, 0, 0),
    (-2, 0, 0, 32, 2, 0, 0),
    (2, 0, 0, 128, -1, 0, 0),
    (-2, 0, 0, 128, 1, 0, 0),
    (2, 0, 0, 64, 0, 1, 0),
    (-2, 0, 0, 64, 0, 1, 0),
    (2, 0, 0, 128, 0, 0, 1),
    (-2, 0, 0, 128, 0, 0, 1),
    (1, 0, 64, 32, -3, 0, 0),
    (-1, 0, 96, 32, 3, 0, 0),
    (1, 0, 0, 128, 0, 1, 0),
    (-1, 0, 0, 128, 0, 1, 0),
    "stats2",
    "stats3",
    (1, 0, 0, 128, 0, 0, 1),
    (-1, 0, 0, 128, 0, 0, 1),
    (2, 1, 64, 32, -2, 0, 0),
    (-2, 1, 96, 32, 2, 0, 0),
    (2, 1, 32, 96, -1, 0, 0),
    (2, 1, 32, 96, -1, 0, 1),
    (2, 1, 0, 128, 0, 0, 1),
    (4, 0, 0, 64, 0, 1, 0),
    (-2, 1, 32, 96, 1, 0, 0),
    (-2, 1, 32, 96, 1, 0, 1),
    (-2, 1, 0, 128, 0, 0, 1),
    (3, 0, 0, 32, 0, 1, 0),
    (3, 0, 0, 32, 0, 1, 1),
    (-3, 0, 0, 32, 0, 1, 0),
    (-3, 0, 0, 32, 0, 1, 1),
    (3, 0, 0, 128, 0, 0, 1),
    (-3, 0, 0, 128, 0, 0, 1),
    (1, 1, 0, 128, 0, 0, 1),
    (4, 0, 0, 128, 0, 0, 1),
    (-1, 1, 0, 128, 0, 0, 1),
    (4, 1, 0, 128, 0, 0, 1),
    "scale",
    0,
    2,
    -2,
    1,
    -1,
    3,
    4,
    -3,
)

NARROW_PLAN = (
    (0, 0, 0, 64, 4, 1, 0),
    (0, 0, 0, 128, -3, 0, 0),
    (0, 0, 0, 128, 3, 0, 0),
    (0, 0, 0, 128, -1, 0, 0),
    (0, 0, 0, 128, 1, 0, 0),
    (0, 0, 0, 128, 0, 1, 0),
    (0, 0, 0, 128, 0, 0, 1),
    "begin",
    (0, 1, 64, 64, 4, 0, 0),
    (0, 1, 0, 128, -2, 0, 0),
    (0, 1, 0, 128, 2, 0, 0),
    (0, 1, 0, 128, -1, 0, 0),
    (0, 1, 0, 128, 1, 0, 0),
    (0, 1, 0, 128, 0, 0, 1),
    0,
    (3, 0, 0, 128, -1, 0, 0),
    (3, 0, 0, 128, 0, 1, 0),
    (3, 0, 0, 128, 0, 0, 1),
    (1, 0, 0, 128, -1, 0, 0),
    (1, 0, 0, 128, -1, 0, 1),
    (1, 0, 0, 128, 0, 0, 1),
    (-3, 0, 0, 128, 0, 1, 0),
    (-3, 0, 0, 128, 0, 1, 1),
    (-3, 0, 0, 128, 0, 0, 1),
    (-1, 0, 0, 128, 1, 0, 0),
    (-1, 0, 0, 128, 1, 0, 1),
    "settle",
    (-1, 0, 0, 128, 0, 0, 1),
    (2, 1, 0, 128, 0, 0, 1),
    (1, 1, 0, 128, 0, 0, 1),
    (3, 1, 0, 128, 0, 0, 1),
    "settle",
    (4, 0, 0, 128, 0, 0, 1),
    (4, 1, 0, 128, 0, 0, 1),
    (-2, 1, 0, 128, 0, 0, 1),
    1,
    (-1, 1, 0, 128, 0, 0, 1),
    3,
    2,
    4,
    -3,
    -1,
    -2,
)


def nearest(dz):
    dz %= Z
    return dz - Z if dz > Z // 2 else dz


class Gather:
    def __init__(self, place, buf, own, plan, send_sem, recv_sem):
        self.p, self.buf, self.own, self.plan = place, buf, own, plan
        self.send_sem, self.recv_sem = send_sem, recv_sem
        self.sends = [step for step in plan if isinstance(step, tuple)]
        self.brings = {}
        for i, (dz, dy, first, rows, tz, ty, tk) in enumerate(self.sends):
            for r in range(first, first + rows, 16):
                self.brings[nearest(dz - tz), dy ^ ty, tk, r] = i
        self.waited = set()
        self.sent = []
        self.settled = 0

    def copy(self, i, block, device):
        p = self.p
        dz, dy, dk = block
        first, rows = self.sends[i][2:4]
        here = self.buf.at[p.along(dz), (p.y + dy) % 2, (p.k + dk) % 2, pl.ds(first, rows)]
        mine = self.own is not None and block == (0, 0, 0)
        return pltpu.make_async_remote_copy(
            src_ref=self.own.at[pl.ds(first, rows)] if mine else here,
            dst_ref=here,
            send_sem=self.send_sem.at[i],
            recv_sem=self.recv_sem.at[i],
            device_id=device,
            device_id_type=MESH,
        )

    def need(self, block, first, rows):
        if block == (0, 0, 0):
            return
        for r in range(first, first + rows, 16):
            i = self.brings[block + (r,)]
            if i not in self.waited:
                self.waited.add(i)
                dz, dy, _, _, tz, ty, tk = self.sends[i]
                self.copy(i, (nearest(dz - tz), dy ^ ty, tk), self.p.to(0, 0, 1)).wait_recv()

    def run(self, on_chip, named):
        for step in self.plan:
            if isinstance(step, str):
                named[step]()
            elif isinstance(step, int):
                for block in ((step, 0, 0), (step, 1, 0), (step, 0, 1), (step, 1, 1)):
                    self.need(block, 0, ROWS)
                on_chip(self.p.along(step))
            else:
                dz, dy, first, rows, tz, ty, tk = step
                self.need((nearest(dz), dy, 0), first, rows)
                c = self.copy(len(self.sent), (dz, dy, 0), self.p.to(tz, ty, tk))
                c.start()
                self.sent.append(c)

    def settle(self, in_flight=0):
        upto = max(self.settled, len(self.sent) - in_flight)
        for c in self.sent[self.settled : upto]:
            c.wait_send()
        self.settled = upto


def kernel(
    tokens,
    gain_hbm,
    in_weight,
    filter_hbm,
    rows_hbm,
    decay_hbm,
    angle_hbm,
    residue_hbm,
    state_hbm,
    skip_hbm,
    out_weight,
    mixed,
    gain,
    short_filter,
    prior_rows,
    decay_rate,
    pole_angle,
    residue,
    skip_weight,
    own,
    wide,
    stats,
    weight,
    narrow,
    last_weight,
    power_re,
    power_im,
    lift_re,
    lift_im,
    response,
    total,
    rim,
    ext,
    padded,
    ends,
    query_out,
    query_in,
    incoming,
    shard_power,
    scales,
    hello,
    local_sem,
    send1,
    recv1,
    send2,
    recv2,
    small_send,
    small_recv,
):
    p = Place()
    barrier = pltpu.get_barrier_semaphore()
    kin = [
        (4 * (p.seq // 4) + (p.seq + 1) % 4, p.chan),
        (4 * (p.seq // 4) + (p.seq + 3) % 4, p.chan),
        ((p.seq + 4) % SEQ, p.chan),
    ]
    greeted = [p.to(*by) for by in ((0, 0, 1), (0, 1, 0), (0, 1, 1), (1, 0, 0), (-1, 0, 0), (2, 0, 0), (-2, 0, 0))]
    greeted += kin
    for device in greeted:
        pl.semaphore_signal(barrier, inc=1, device_id=device, device_id_type=MESH)

    pairs = (
        (tokens, own),
        (gain_hbm, gain),
        (filter_hbm, short_filter),
        (rows_hbm, prior_rows),
        (decay_hbm, decay_rate),
        (angle_hbm, pole_angle),
        (residue_hbm, residue),
        (state_hbm, incoming),
        (skip_hbm, skip_weight),
    )
    loads = [pltpu.make_async_copy(a, b, local_sem.at[4 + i]) for i, (a, b) in enumerate(pairs)]
    weight_loads = []
    for i in range(3):
        weight_loads.append(
            pltpu.make_async_copy(in_weight.at[i], weight.at[:, pl.ds(i * CH, CH)], local_sem.at[i])
        )
    last_load = pltpu.make_async_copy(out_weight, last_weight, local_sem.at[3])
    for c in loads + weight_loads + [last_load]:
        c.start()

    pl.semaphore_wait(barrier, len(greeted))

    def small(src, dst, index, device):
        return pltpu.make_async_remote_copy(
            src_ref=src,
            dst_ref=dst,
            send_sem=small_send.at[index],
            recv_sem=small_recv.at[index],
            device_id=device,
            device_id_type=MESH,
        )

    small_sent = []

    def spread_small(src, index, device):
        c = small(src, src, index, device)
        c.start()
        small_sent.append(c)

    def small_here(z, index):
        small(stats.at[z], stats.at[z], index, p.to(0, 0, 1)).wait_recv()

    pair = ((0, 1), (1, 0), (1, 1))

    def stats1():
        loads[0].wait()
        loads[1].wait()
        values = own[...].astype(F32)
        squares = jnp.sum(values * values, axis=1, keepdims=True)
        row = jnp.broadcast_to(squares, (ROWS, 128)).T
        gains = gain[...].astype(F32).reshape(1, FEATS)
        stats[p.z, 2 * p.y + p.k] = jnp.concatenate(
            [row[0:1], gains[:, 0:128], gains[:, 128:256], row[3:4]], axis=0
        )
        wide[p.z, p.y, p.k] = own[...]
        for i, (dy, dk) in enumerate(pair):
            spread_small(stats.at[p.z, 2 * p.y + p.k], i, p.to(0, dy, dk))
        for device in kin:
            pl.semaphore_signal(hello.at[0], inc=1, device_id=device, device_id_type=MESH)

    def stats2():
        for i, (dy, dk) in enumerate(pair):
            theirs = stats.at[p.z, 2 * ((p.y + dy) % 2) + (p.k + dk) % 2]
            small(theirs, theirs, i, p.to(0, dy, dk)).wait_recv()
        for i, by in enumerate((1, -1, 2, -2)):
            spread_small(stats.at[p.z], 3 + i, p.to(by, 0, 0))

    def stats3():
        for i, by in enumerate((3, -3, 4)):
            spread_small(stats.at[p.z], 7 + i, p.to(by, 0, 0))

    def tables():
        for c in loads[2:]:
            c.wait()
        magnitude = jnp.exp(-decay_rate[...])
        pole_re = magnitude * jnp.cos(pole_angle[...])
        pole_im = magnitude * jnp.sin(pole_angle[...])
        res_re = residue[0]
        res_im = residue[1]

        def tabulate(t, carry):
            re, im, lre, lim = carry
            power_re[t] = re
            power_im[t] = im
            response[pl.ds(8 + t, 1)] = jnp.sum(lre, axis=0, keepdims=True)
            lre, lim = pole_re * lre - pole_im * lim, pole_re * lim + pole_im * lre
            lift_re[t] = lre
            lift_im[t] = lim
            return (pole_re * re - pole_im * im, pole_re * im + pole_im * re, lre, lim)

        one = jnp.ones((MODES, CH), F32)
        end_re, end_im, _, _ = lax.fori_loop(
            0, ROWS, tabulate, (one, jnp.zeros_like(one), res_re, res_im)
        )
        padded[pl.ds(0, ROWS)] = jnp.zeros((ROWS, CH), F32)
        response[pl.ds(0, 8)] = jnp.zeros((8, CH), F32)
        total[...] = jnp.zeros_like(total)
        shard_power[0] = end_re
        shard_power[1] = end_im

    def find_scale():
        for i, by in enumerate((1, -1, 2, -2, 3, -3, 4)):
            small_here(p.along(-by), 3 + i)
        pl.semaphore_wait(hello.at[0], len(kin))
        for device in kin:
            pl.semaphore_signal(hello.at[1], inc=1, device_id=device, device_id_type=MESH)
        summed = jnp.zeros((1, 128), F32)
        for z in range(Z):
            for j in range(4):
                summed = summed + stats[z, j, 0:1]
        scale_row = lax.rsqrt(summed / (FEATS * 4 * Z) + EPSILON)
        scales[...] = jnp.broadcast_to(scale_row, (ROWS, 128)).T
        for c in weight_loads:
            c.wait()

    def project(z):
        parts = []
        scale = scales[...]
        for j in range(4):
            x = wide[z, j // 2, j % 2].astype(F32)
            for h in range(2):
                part = x[:, 128 * h : 128 * h + 128] * scale * stats[z, j, 1 + h : 2 + h]
                parts.append(part.astype(BF16))
        normed = jnp.concatenate(parts, axis=1)
        rows = weight[pl.ds(pl.multiple_of(z * 4 * FEATS, 4 * FEATS), 4 * FEATS)]
        total[...] += jnp.dot(normed, rows, preferred_element_type=F32)

    spread = Gather(p, wide, tokens, WIDE_PLAN, send1, recv1)
    spread.run(
        project,
        {"stats1": stats1, "tables": tables, "stats2": stats2, "stats3": stats3, "scale": find_scale},
    )

    def close_spread():
        for c in small_sent:
            c.wait_send()
        spread.settle()

    projected = total[...].astype(BF16).astype(F32)
    ext[pl.ds(0, 8)] = jnp.zeros((8, 3 * CH), F32)
    ext[pl.ds(8, ROWS)] = projected

    def convolve(i):
        lanes = pl.ds(i * CH, CH)
        c = jnp.zeros((ROWS, CH), F32)
        for lag in range(3):
            c = c + short_filter[lag, i : i + 1] * ext[pl.ds(8 - lag, ROWS), lanes]
        return c

    key, value = convolve(1), convolve(2)
    row_of = lax.broadcasted_iota(jnp.int32, (ROWS, CH), 0)
    drive = jnp.where(row_of < 2, 0.0, key * value)
    padded[pl.ds(ROWS, ROWS)] = drive

    nothing = jnp.zeros((MODES, CH), F32)
    sums = [[nothing, nothing] for _ in range(4)]
    for t in range(2, ROWS):
        u = padded[pl.ds(ROWS + t, 1)]
        sums[t % 4][0] += power_re[ROWS - 1 - t] * u
        sums[t % 4][1] += power_im[ROWS - 1 - t] * u

    edges = [projected[ROWS - 2 :, i * CH : i * CH + CH] for i in (1, 2)] + [key[0:2], value[0:2]]
    ends[p.seq, pl.ds(0, MODES)] = sums[0][0] + sums[1][0] + sums[2][0] + sums[3][0]
    ends[p.seq, pl.ds(MODES, MODES)] = sums[0][1] + sums[1][1] + sums[2][1] + sums[3][1]
    ends[p.seq, pl.ds(2 * MODES, 8)] = jnp.concatenate(edges, axis=0)
    here = ends.at[p.seq]

    def end_copy(i):
        return small(here, here, 10 + i, ((p.seq + i) % SEQ, p.chan))

    pl.semaphore_wait(hello.at[1], len(kin))
    for i in (6, 5, 7, 4, 2, 3, 1):

        @pl.when(p.seq + i < SEQ)
        def _():
            end_copy(i).start()

    query_out[...] = projected[ROWS - 8 :, 0:CH]
    query_copy = small(query_out, query_in, 10, ((p.seq + 1) % SEQ, p.chan))

    @pl.when(p.seq < SEQ - 1)
    def _():
        query_copy.start()

    def close_state():
        @pl.when(p.seq < SEQ - 1)
        def _():
            query_copy.wait_send()

        for i in range(1, SEQ):

            @pl.when(p.seq + i < SEQ)
            def _():
                end_copy(i).wait_send()

    query = convolve(0)

    def respond(i, acc):
        for j in range(4):
            lag = 4 * i + j
            acc = acc + response[pl.ds(8 + lag, 1)] * padded[pl.ds(ROWS - lag, ROWS)]
        return acc

    mode_out = lax.fori_loop(0, ROWS // 4, respond, jnp.zeros((ROWS, CH), F32))
    def first_rows(i, so_far):
        near, far = short_filter[1, i : i + 1], short_filter[2, i : i + 1]
        before = rim[pl.ds(2 * i, 2)]
        return (
            so_far[0:1] + near * before[1:2] + far * before[0:1],
            so_far[1:2] + far * before[1:2],
        )

    def first_drive(key_rows, value_rows):
        (key0, key1), (value0, value1) = first_rows(1, key_rows), first_rows(2, value_rows)
        return key0 * value0, key1 * value1

    for i in range(3):
        rim[pl.ds(2 * i, 2)] = prior_rows[i].astype(F32)

    @pl.when(p.seq > 0)
    def _():
        query_copy.wait_recv()
        rim[pl.ds(0, 2)] = query_in[pl.ds(6, 2)]

    shard_re, shard_im = shard_power[0], shard_power[1]
    last_re, last_im = power_re[ROWS - 1], power_im[ROWS - 1]
    next_re, next_im = power_re[ROWS - 2], power_im[ROWS - 2]
    for j in range(SEQ - 1):

        @pl.when(j < p.seq)
        def _():
            theirs = ends.at[j]
            for i in range(1, SEQ):

                @pl.when(p.seq - j == i)
                def _():
                    small(theirs, theirs, 10 + i, (j, p.chan)).wait_recv()

            drive0, drive1 = first_drive(ends[j, pl.ds(36, 2)], ends[j, pl.ds(38, 2)])
            re, im = incoming[0], incoming[1]
            end_re = ends[j, pl.ds(0, MODES)] + last_re * drive0 + next_re * drive1
            end_im = ends[j, pl.ds(MODES, MODES)] + last_im * drive0 + next_im * drive1
            incoming[0] = shard_re * re - shard_im * im + end_re
            incoming[1] = shard_re * im + shard_im * re + end_im
            rim[pl.ds(2, 4)] = ends[j, pl.ds(32, 4)]

    in_re, in_im = incoming[0], incoming[1]
    carried = []
    for b in range(ROWS // 8):
        lre = lift_re[pl.ds(8 * b, 8)]
        lim = lift_im[pl.ds(8 * b, 8)]
        carried.append(jnp.sum(lre * in_re[None] - lim * in_im[None], axis=1))
    drive0, drive1 = first_drive(key[0:2], value[0:2])
    query0, query1 = first_rows(0, query[0:2])
    first, second = row_of == 0, row_of == 1
    drive = jnp.where(first, drive0, jnp.where(second, drive1, drive))
    query = jnp.where(first, query0, jnp.where(second, query1, query))
    mode_out = mode_out + response[pl.ds(8, ROWS)] * drive0 + response[pl.ds(7, ROWS)] * drive1
    mode_out = mode_out + jnp.concatenate(carried, axis=0)
    narrow[p.z, p.y, p.k] = (query * (mode_out + skip_weight[...] * drive)).astype(BF16)

    def begin():
        total[:, pl.ds(0, FEATS)] = own[...].astype(F32)
        last_load.wait()

    def output(z):
        parts = [narrow[z, j // 2, j % 2] for j in range(4)]
        rows = last_weight[pl.ds(pl.multiple_of(z * 4 * CH, 4 * CH), 4 * CH)]
        total[:, pl.ds(0, FEATS)] += jnp.dot(
            jnp.concatenate(parts, axis=1), rows, preferred_element_type=F32
        )

    mix = Gather(p, narrow, None, NARROW_PLAN, send2, recv2)

    def settle():
        if not mix.settled:
            close_state()
            close_spread()
        mix.settle(in_flight=8)

    mix.run(output, {"begin": begin, "settle": settle})
    mixed[...] = total[:, pl.ds(0, FEATS)].astype(BF16)

    mix.settle()


def body(
    tokens,
    norm_gain,
    in_weight,
    short_filter,
    prior_rows,
    decay_rate,
    pole_angle,
    residue,
    prior_state,
    skip_weight,
    out_weight,
):
    vmem = pl.BlockSpec(memory_space=pltpu.VMEM)
    hbm = pl.BlockSpec(memory_space=pltpu.HBM)
    flops = 2 * ROWS * (FEATS * 32 * 3 * CH + CH * 32 * FEATS)
    return pl.pallas_call(
        kernel,
        out_shape=jax.ShapeDtypeStruct((ROWS, FEATS), BF16),
        in_specs=[hbm] * 11,
        out_specs=vmem,
        scratch_shapes=[
            pltpu.VMEM((FEATS,), BF16),
            pltpu.VMEM((3, 3, CH), F32),
            pltpu.VMEM((3, 2, CH), BF16),
            pltpu.VMEM((MODES, CH), F32),
            pltpu.VMEM((MODES, CH), F32),
            pltpu.VMEM((2, MODES, CH), F32),
            pltpu.VMEM((1, CH), F32),
            pltpu.VMEM((ROWS, FEATS), BF16),
            pltpu.VMEM((Z, 2, 2, ROWS, FEATS), BF16),
            pltpu.VMEM((Z, 4, 4, 128), F32),
            pltpu.VMEM((Z * 4 * FEATS, 3 * CH), BF16),
            pltpu.VMEM((Z, 2, 2, ROWS, CH), BF16),
            pltpu.VMEM((Z * 4 * CH, FEATS), BF16),
            pltpu.VMEM((ROWS, MODES, CH), F32),
            pltpu.VMEM((ROWS, MODES, CH), F32),
            pltpu.VMEM((ROWS, MODES, CH), F32),
            pltpu.VMEM((ROWS, MODES, CH), F32),
            pltpu.VMEM((8 + ROWS, CH), F32),
            pltpu.VMEM((ROWS, 3 * CH), F32),
            pltpu.VMEM((8, CH), F32),
            pltpu.VMEM((8 + ROWS, 3 * CH), F32),
            pltpu.VMEM((2 * ROWS, CH), F32),
            pltpu.VMEM((SEQ, 2 * MODES + 8, CH), F32),
            pltpu.VMEM((8, CH), F32),
            pltpu.VMEM((8, CH), F32),
            pltpu.VMEM((2, MODES, CH), F32),
            pltpu.VMEM((2, MODES, CH), F32),
            pltpu.VMEM((ROWS, 128), F32),
            pltpu.SemaphoreType.REGULAR((2,)),
            pltpu.SemaphoreType.DMA((13,)),
            pltpu.SemaphoreType.DMA((len(WIDE_PLAN),)),
            pltpu.SemaphoreType.DMA((len(WIDE_PLAN),)),
            pltpu.SemaphoreType.DMA((len(NARROW_PLAN),)),
            pltpu.SemaphoreType.DMA((len(NARROW_PLAN),)),
            pltpu.SemaphoreType.DMA((18,)),
            pltpu.SemaphoreType.DMA((18,)),
        ],
        compiler_params=pltpu.CompilerParams(
            collective_id=0, has_side_effects=True, vmem_limit_bytes=60 * 1024 * 1024
        ),
        cost_estimate=pl.CostEstimate(flops=flops, bytes_accessed=9 * 1024 * 1024, transcendentals=0),
    )(
        tokens,
        norm_gain,
        jnp.transpose(in_weight, (1, 0, 2)),
        short_filter,
        jnp.transpose(prior_rows, (1, 0, 2)),
        decay_rate.T,
        pole_angle.T,
        jnp.transpose(residue, (0, 2, 1)),
        jnp.transpose(prior_state, (0, 2, 1)),
        skip_weight.reshape(1, CH),
        out_weight,
    )


def solution(mesh):
    return jax.shard_map(
        body,
        mesh=mesh,
        in_specs=(
            P("seq", "chan"),
            P("chan"),
            P(None, None, "chan"),
            P(None, None, "chan"),
            P(None, None, "chan"),
            P("chan", None),
            P("chan", None),
            P(None, "chan", None),
            P(None, "chan", None),
            P("chan"),
            P(None, "chan"),
        ),
        out_specs=P("seq", "chan"),
        check_vma=False,
    )
```
